256 devices in a mesh: dp: 128 (over z, y, x), rep: 2 (over core).
Axes of the slice: x: 4, y: 4, z: 8, core: 2. Of those that a mesh axis runs over, the one named last changes fastest.
Arguments:
- activations: bfloat16 [188416, 4096], P(('dp', 'rep')), may hold values from -24 to 24
- out_grads: bfloat16 [188416, 512], P(('dp', 'rep')), may hold values from -6 to 6
- worker_error: bfloat16 [128, 4096, 512], P('dp', 'rep'), may hold values from -3 to 3
- momentum_codes: bfloat16 [4096, 512], P(('rep', 'dp')), may hold values from -1 to 1
- momentum_scale: float32 [4096], P(('rep', 'dp')), may hold values from 1 to 4
- server_error: float32 [4096, 512], P(('rep', 'dp')), may hold values from -0.6 to 0.6
- master_weight: float32 [4096, 512], P(('rep', 'dp')), may hold values from -4 to 4
- variance: float32 [4096, 512], P(('rep', 'dp')), may hold values from 0.001 to 1
Outputs:
- next_worker: bfloat16 [128, 4096, 512], P('dp', 'rep')
- next_codes: bfloat16 [4096, 512], P(('rep', 'dp'))
- next_scale: float32 [4096], P(('rep', 'dp'))
- next_server: float32 [4096, 512], P(('rep', 'dp'))
- next_master: float32 [4096, 512], P(('rep', 'dp'))
- weights_full: bfloat16 [4096, 512], P('rep')
The draws below stay inside these ranges and needn't reach their ends.
All inputs are finite; a program needn't handle non-finite values. Where the reference program divides by a largest or mean magnitude, that divisor is 1e-20 or more.
Results may differ from the reference program's by a relative error of at most 0.012.
Values may be sent and summed in bfloat16 or wider, within the bound.
A program may use at most 128 MiB of HBM per device.

```python
import math
import jax
import jax.numpy as jnp
from jax import lax

D = 4096
KV_WIDTH = 512
TOK_DEV = 736
TOKENS = 188416
N_DP = 128
N_REP = 2


def raised(entries, rng, source, target, blocks, factor):
    owner, partner = [(jnp.arange(entries.shape[axis_at]) // (entries.shape[axis_at] // blocks)).reshape([-1 if axis == axis_at else 1 for axis in range(entries.ndim)]) for axis_at in (source, target)]
    chosen = jax.random.permutation(rng, blocks)[partner]
    strong = (owner == chosen) | (owner == (partner + blocks // 2) % blocks)
    return jnp.where(strong, factor * entries, entries)


def block_levels(key, shape, shards, low, largest):
    loudness = 1.0
    for position, blocks in shards:
        heights = jax.random.uniform(jax.random.fold_in(jax.random.fold_in(key, 6), position), (blocks,), jnp.float32, low / len(shards), largest / len(shards))
        loudness = loudness * jnp.repeat(jnp.exp(heights), shape[position] // blocks).reshape((-1,) + (1,) * (len(shape) - 1 - position))
    return loudness


def normal_values(stream_key, dims, width, limit, pieces=(), held_as=jnp.bfloat16):
    entries = jax.random.normal(stream_key, dims, jnp.float32) * width
    if len(pieces) > 0:
        entries = block_levels(stream_key, dims, pieces, -0.22, 0.18) * entries
    return jnp.clip(entries, min=-limit, max=limit).astype(held_as)


def noise_with(stream_key, shape, width, most, shards, heavy, kind=jnp.bfloat16):
    result = width * jax.random.normal(stream_key, shape, jnp.float32)
    if shards:
        result = result * block_levels(stream_key, shape, shards, -0.22, 0.18)
    return jnp.clip(raised(result, jax.random.fold_in(stream_key, 3), *heavy), -most, most).astype(kind)


def setup_inputs(seed: int = 0) -> dict:
    splits = jax.random.split(jax.random.key(seed), 9)
    activations = noise_with(splits[0], (TOKENS, D), 1.0, 24.0, ((0, 256),), (0, 1, 256, 6.0))
    out_grads = normal_values(splits[1], (TOKENS, KV_WIDTH), 1.0, 6.0, ((0, 256),))
    worker_error = normal_values(splits[2], (N_DP, D, KV_WIDTH), 0.5, 3.0, ((0, 128), (1, 2)))
    momentum_codes = jnp.clip(jax.random.uniform(splits[3], (D, KV_WIDTH), jnp.float32, -1.0, 1.0) * block_levels(splits[3], (D, KV_WIDTH), ((0, 256),), -0.4, 0.0), -1.0, 1.0).astype(jnp.bfloat16)
    momentum_scale = jnp.clip(jnp.exp(math.log(4.0) - 1.3862944 * jax.random.uniform(splits[4], (D,), jnp.float32) ** block_levels(splits[4], (D,), ((0, 256),), -0.2, 0.2)), 1.0, 4.0)
    server_error = normal_values(splits[5], (D, KV_WIDTH), 0.1, 0.6, ((0, 256),), jnp.float32)
    master_weight = normal_values(splits[6], (D, KV_WIDTH), 1.0, 4.0, ((0, 256),), jnp.float32)
    variance = jnp.clip(jnp.exp(math.log(1.0) - 6.9077552 * jax.random.uniform(splits[7], (D, KV_WIDTH), jnp.float32) ** block_levels(splits[7], (D, KV_WIDTH), ((0, 256),), -0.2, 0.2)), 0.001, 1.0)
    return {"activations": activations, "out_grads": out_grads, "worker_error": worker_error, "momentum_codes": momentum_codes, "momentum_scale": momentum_scale, "server_error": server_error, "master_weight": master_weight, "variance": variance}


beta_one = 0.9
learn_rate = 0.02
grad_boost = 8.0
tiny_scale = 1e-06
tiny_root = 1e-08

def compress_rows(values):
    row_scale = lax.optimization_barrier(jnp.mean(jnp.abs(values), axis=1)) + tiny_scale
    row_codes = jnp.clip(values / row_scale[:, None], -1.0, 1.0).astype(jnp.bfloat16)
    return (row_codes, row_scale)

def reference(activations, out_grads, worker_error, momentum_codes, momentum_scale, server_error, master_weight, variance):
    chip_rows = N_REP * TOK_DEV
    grad_factor = grad_boost / math.sqrt(chip_rows)
    previous = momentum_codes.astype(jnp.float32) * momentum_scale[:, None]

    def one_chip(running, chip_index):
        row_start = (chip_index * chip_rows).astype(jnp.int32)
        rows_in = lax.dynamic_slice_in_dim(activations, row_start, chip_rows, 0)
        rows_grad = lax.dynamic_slice_in_dim(out_grads, row_start, chip_rows, 0)
        gradient = jnp.dot(rows_in.T, rows_grad, preferred_element_type=jnp.float32) * grad_factor
        chip_error = lax.dynamic_index_in_dim(worker_error, chip_index, 0, keepdims=False)
        combined = beta_one * previous + (1.0 - beta_one) * gradient + chip_error.astype(jnp.float32)
        row_codes, row_scale = compress_rows(combined)
        decoded = row_codes.astype(jnp.float32) * row_scale[:, None]
        leftover = (combined - decoded).astype(jnp.bfloat16)
        return (running + decoded, leftover)
    running, next_worker = lax.scan(one_chip, jnp.zeros((D, KV_WIDTH), jnp.float32), jnp.arange(N_DP, dtype=jnp.int32))
    average = running / N_DP
    shifted = average + server_error
    next_codes, next_scale = compress_rows(shifted)
    momentum = next_codes.astype(jnp.float32) * next_scale[:, None]
    next_server = shifted - momentum
    next_master = master_weight - learn_rate * momentum / (jnp.sqrt(variance) + tiny_root)
    return (next_worker, next_codes, next_scale, next_server, next_master, next_master.astype(jnp.bfloat16))
```

```python
import math

import jax
import jax.numpy as jnp
from jax import lax
from jax.experimental import pallas as pl
from jax.experimental.pallas import tpu as pltpu
from jax.sharding import PartitionSpec as P

BF16 = jnp.bfloat16
F32 = jnp.float32
MESH = pl.DeviceIdType.MESH

NX, NY, NZ = 4, 4, 8
OWN = 16
LANES = 128
CHUNK = 256
HALF = 2048
WIDTH = 512
CHUNKS = HALF // CHUNK

beta_one = 0.9
learn_rate = 0.02
grad_boost = 8.0
tiny_scale = 1e-06
tiny_root = 1e-08


class Links:
    def __init__(self, send_sems, recv_sems, core):
        self.send_sems, self.recv_sems, self.core = send_sems, recv_sems, core
        self.used = 0
        self.open = []

    def sem(self):
        self.used += 1
        return self.used - 1

    def send(self, src, dst, sem, dp, rep=None):
        copy = pltpu.make_async_remote_copy(
            src_ref=src,
            dst_ref=dst,
            send_sem=self.send_sems.at[sem],
            recv_sem=self.recv_sems.at[sem],
            device_id={"dp": dp, "rep": self.core if rep is None else rep},
            device_id_type=MESH,
        )
        copy.start()
        self.open.append(copy)

    def arrived(self, dst, sem, dp):
        pltpu.make_async_remote_copy(
            src_ref=dst,
            dst_ref=dst,
            send_sem=self.send_sems.at[sem],
            recv_sem=self.recv_sems.at[sem],
            device_id={"dp": dp, "rep": self.core},
            device_id_type=MESH,
        ).wait_recv()

    def drain(self):
        for copy in self.open:
            copy.wait_send()
        self.open = []


class Ring:
    def __init__(self, links, size, me, dp_at):
        self.links, self.size, self.me, self.dp_at = links, size, me, dp_at
        self.reach = size // 2
        self.sems = {}
        for hop in range(1, self.reach + 1):
            for way in (1, -1):
                for half in (0, 1):
                    self.sems[way, hop, half] = links.sem()

    def at(self, offset):
        return lax.rem(self.me + (offset + self.size), self.size)

    def first(self, way):
        return 0 if way == 1 else 1

    def plan(self):
        for turn in (0, 1):
            for way in (1, -1):
                yield turn, way, self.first(way) if turn == 0 else 1 - self.first(way)

    def gather_hop(self, view, hop):
        for turn, way, half in self.plan():
            if hop == self.reach and turn == 1:
                continue
            part = view(self.at(-way * (hop - 1)), half)
            if hop > 1:
                self.links.arrived(part, self.sems[way, hop - 1, half], self.dp_at(self.at(-way)))
            self.links.send(part, part, self.sems[way, hop, half], self.dp_at(self.at(way)))

    def gather_end(self, view):
        for turn, way, half in self.plan():
            if turn == 1:
                hop = self.reach - 1
                part = view(self.at(-way * hop), half)
                self.links.arrived(part, self.sems[way, hop, half], self.dp_at(self.at(-way)))
        for turn, way, half in self.plan():
            if turn == 0:
                hop = self.reach
                part = view(self.at(-way * hop), half)
                self.links.arrived(part, self.sems[way, hop, half], self.dp_at(self.at(-way)))

    def reduce_begin(self, view, slot):
        for turn, way, half in self.plan():
            hop = 1 if turn == 0 else 2
            self.links.send(
                view(self.at(way * (self.reach - hop + 1)), half),
                slot(way, hop, half),
                self.sems[way, hop, half],
                self.dp_at(self.at(way)),
            )

    def reduce_hop(self, view, slot, hop):
        for turn, way, half in self.plan():
            if hop == 2 and turn == 1:
                continue
            got = slot(way, hop - 1, half)
            self.links.arrived(got, self.sems[way, hop - 1, half], self.dp_at(self.at(-way)))
            part = view(self.at(way * (self.reach - hop + 1)), half)
            part[...] = (part[...].astype(F32) + got[...].astype(F32)).astype(BF16)
            self.links.send(
                part, slot(way, hop, half), self.sems[way, hop, half], self.dp_at(self.at(way))
            )

    def reduce_end(self, slot):
        for turn, way, half in self.plan():
            self.links.arrived(
                slot(way, self.reach, half),
                self.sems[way, self.reach, half],
                self.dp_at(self.at(-way)),
            )


class Part:
    def __init__(self, links, sizes, place, dp_of):
        self.links = links
        self.n_last, self.n_mid, self.n_first = sizes
        self.last, self.mid, self.first = place
        self.dp_of = dp_of

    def dp_last(self, j):
        return self.dp_of(j, self.mid, self.first)

    def dp_mid(self, j):
        return self.dp_of(self.last, j, self.first)

    def dp_first(self, j):
        return self.dp_of(self.last, self.mid, j)

    def first_at(self, offset):
        return lax.rem(self.first + (offset + self.n_first), self.n_first)

    def last_view(self, buf):
        step = self.n_mid // 2
        return lambda j, half: buf.at[j, pl.ds(half * step, step)]

    def mid_view(self, buf):
        step = self.n_first // 2
        return lambda j, half: buf.at[self.last, j, pl.ds(half * step, step)]

    def gather_first(self, buf):
        self.first_sems = [self.links.sem() for _ in range(1, self.n_first)]
        mine = buf.at[self.last, self.mid, self.first]
        for k in range(1, self.n_first):
            self.links.send(mine, mine, self.first_sems[k - 1], self.dp_first(self.first_at(k)))

    def gather_mid(self, buf):
        for k in range(1, self.n_first):
            j = self.first_at(-k)
            self.links.arrived(
                buf.at[self.last, self.mid, j], self.first_sems[k - 1], self.dp_first(j)
            )
        self.ring = Ring(self.links, self.n_mid, self.mid, self.dp_mid)
        self.ring.gather_hop(self.mid_view(buf), 1)

    def gather_mid_relay(self, buf):
        self.ring.gather_hop(self.mid_view(buf), 2)

    def gather_last(self, buf):
        self.ring.gather_end(self.mid_view(buf))
        self.ring = Ring(self.links, self.n_last, self.last, self.dp_last)
        self.ring.gather_hop(self.last_view(buf), 1)

    def gather_last_relay(self, buf, hop):
        if hop <= self.ring.reach:
            self.ring.gather_hop(self.last_view(buf), hop)

    def gather_end(self, buf):
        self.ring.gather_end(self.last_view(buf))

    def reduce_last(self, dec, got):
        step = self.n_mid // 2
        self.got = lambda way, hop, half: got.at[
            0 if way == 1 else 1, hop - 1, pl.ds(half * step, step)
        ]
        self.ring = Ring(self.links, self.n_last, self.last, self.dp_last)
        self.ring.reduce_begin(self.last_view(dec), self.got)

    def reduce_last_relay(self, dec, hop):
        if hop <= self.ring.reach:
            self.ring.reduce_hop(self.last_view(dec), self.got, hop)

    def reduce_mid(self, dec, got, partial, got_mid):
        reach = self.ring.reach
        self.ring.reduce_end(self.got)
        for j in range(self.n_mid):
            total = dec[self.last, j].astype(F32)
            total += got[0, reach - 1, j].astype(F32) + got[1, reach - 1, j].astype(F32)
            partial[j] = total.astype(BF16)
        step = self.n_first // 2
        self.got_mid = lambda way, hop, half: got_mid.at[
            0 if way == 1 else 1, hop - 1, pl.ds(half * step, step)
        ]
        self.partial_view = lambda j, half: partial.at[j, pl.ds(half * step, step)]
        self.ring = Ring(self.links, self.n_mid, self.mid, self.dp_mid)
        self.ring.reduce_begin(self.partial_view, self.got_mid)

    def reduce_mid_relay(self):
        self.ring.reduce_hop(self.partial_view, self.got_mid, 2)

    def reduce_first(self, partial, got_mid, sums, got_first):
        self.ring.reduce_end(self.got_mid)
        sums[...] = partial[self.mid].astype(F32) + (
            got_mid[0, 1].astype(F32) + got_mid[1, 1].astype(F32)
        )
        self.first_sems = [self.links.sem() for _ in range(1, self.n_first)]
        for k in range(1, self.n_first):
            j = self.first_at(k)
            self.links.send(
                sums.at[j], got_first.at[k - 1], self.first_sems[k - 1], self.dp_first(j)
            )

    def reduce_end(self, sums, got_first):
        total = sums[self.first]
        for k in range(1, self.n_first):
            self.links.arrived(
                got_first.at[k - 1], self.first_sems[k - 1], self.dp_first(self.first_at(-k))
            )
        for k in range(1, self.n_first):
            total += got_first[k - 1]
        return total


def step_kernel(
    act, grads, werr, mcodes, mscale, serr, master, variance,
    left_out, codes_out, scale_out, server_out, master_out, weights_out,
    act_v, grads_v, werr_v, mcodes_v, serr_v, master_v, variance_v,
    left_v, codes_v, server_v, new_master_v,
    own_g, peer_tx, peer_rx,
    mom, mom_c, dec, dec_c, wts, wts_c,
    got, got_c, partial, partial_c, got_mid, got_mid_c, sums, sums_c, got_first, got_first_c,
    in_sems, act_sems, out_sems, peer_send, peer_recv, send_sems, recv_sems,
):
    dp = lax.axis_index("dp")
    core = lax.axis_index("rep")
    x = lax.rem(dp, NX)
    y = lax.rem(dp // NX, NY)
    z = dp // (NX * NY)
    other = 1 - core
    tokens = act.shape[0]
    factor = (1.0 - beta_one) * grad_boost / math.sqrt(2 * tokens)

    def load(k, src, dst):
        copy = pltpu.make_async_copy(src, dst, in_sems.at[k])
        copy.start()
        return copy

    load_codes = load(0, mcodes, mcodes_v)
    load_grads = load(1, grads, grads_v)

    def act_copy(k):
        base = jnp.where(k < CHUNKS, other * HALF, core * HALF)
        column = pl.multiple_of(base + lax.rem(k, CHUNKS) * CHUNK, CHUNK)
        return pltpu.make_async_copy(
            act.at[:, pl.ds(column, CHUNK)], act_v.at[k], act_sems.at[k]
        )

    @pl.loop(0, 2 * CHUNKS)
    def _(k):
        act_copy(k).start()

    load_werr = load(2, werr, werr_v)
    load_serr = load(3, serr, serr_v)
    load_master = load(4, master, master_v)
    load_variance = load(5, variance, variance_v)

    def dp_at(zz, yy, xx):
        return zz * (NX * NY) + yy * NX + xx

    barrier = pltpu.get_barrier_semaphore()
    peers = [(dp_at(lax.rem(z + k, NZ), y, x), core) for k in range(1, NZ)]
    peers += [(dp_at(z, y, lax.rem(x + k, NX)), core) for k in range(1, NX)]
    peers += [(dp_at(z, lax.rem(y + k, NY), x), core) for k in (1, NY - 1)]
    peers += [(dp, other)]
    for peer_dp, peer_core in peers:
        pl.semaphore_signal(
            barrier, inc=1, device_id={"dp": peer_dp, "rep": peer_core}, device_id_type=MESH
        )

    eye = lax.broadcasted_iota(jnp.int32, (OWN, OWN), 0) == lax.broadcasted_iota(
        jnp.int32, (OWN, OWN), 1
    )
    scale_col = jnp.sum(
        jnp.where(eye, jnp.broadcast_to(mscale[...], (OWN, OWN)), 0.0), axis=1, keepdims=True
    )
    load_codes.wait()
    previous = (mcodes_v[...].astype(F32) * scale_col).astype(BF16)

    links = Links(send_sems, recv_sems, core)
    def mixed(a, b):
        return a + core * (b - a)

    part_x = Part(links, (NX, NY, NZ), (x, y, z), lambda l, m, f: dp_at(f, m, l))
    part_y = Part(links, (NY, NX, NZ), (y, x, z), lambda l, m, f: dp_at(f, l, m))
    part_m = Part(
        links,
        (NX, NY, NZ),
        (mixed(x, y), mixed(y, x), z),
        lambda l, m, f: dp_at(f, mixed(m, l), mixed(l, m)),
    )
    part_z = Part(links, (NZ, NY, NX), (z, y, x), lambda l, m, f: dp_at(l, m, f))
    parts = [part_z, part_x, part_y, part_m]

    def bufs(three, one):
        return [one, three.at[0], three.at[1], three.at[2]]

    def columns(q):
        return slice(q * LANES, (q + 1) * LANES)

    quarter = [3, 0, 1, 2]

    moms = bufs(mom, mom_c)
    for part, buf, q in zip(parts, moms, quarter):
        buf[part.last, part.mid, part.first] = previous[:, columns(q)]
    pl.semaphore_wait(barrier, len(peers))

    for part, buf in zip(parts, moms):
        part.gather_first(buf)

    def product(k):
        act_copy(k).wait()
        return lax.dot_general(
            act_v[k], grads_v[...], (((0,), (0,)), ((), ())), preferred_element_type=F32
        )

    def chunk_rows(k):
        return pl.ds(pl.multiple_of(k * CHUNK, CHUNK), CHUNK)

    def peer_copy(k):
        rows = chunk_rows(k)
        return pltpu.make_async_remote_copy(
            src_ref=peer_tx.at[rows],
            dst_ref=peer_rx.at[rows],
            send_sem=peer_send.at[k],
            recv_sem=peer_recv.at[k],
            device_id={"dp": dp, "rep": other},
            device_id_type=MESH,
        )

    def for_other(lo, hi):
        @pl.loop(lo, hi)
        def _(k):
            peer_tx[chunk_rows(k)] = product(k).astype(BF16)
            peer_copy(k).start()

    def for_own(lo, hi):
        @pl.loop(lo, hi)
        def _(k):
            own_g[chunk_rows(k)] = product(k + CHUNKS)

    load_grads.wait()
    for_other(0, 4)
    for part, buf in zip(parts, moms):
        part.gather_mid(buf)
    for_other(4, 6)
    for part, buf in zip(parts, moms):
        part.gather_mid_relay(buf)
    for_other(6, 8)
    for part, buf in zip(parts, moms):
        part.gather_last(buf)
    for_own(0, 3)
    for part, buf in zip(parts, moms):
        part.gather_last_relay(buf, 2)
    for_own(3, 6)
    part_z.gather_last_relay(mom_c, 3)
    for_own(6, 8)
    part_z.gather_last_relay(mom_c, 4)

    load_werr.wait()

    @pl.loop(0, CHUNKS)
    def _(k):
        peer_copy(k).wait_recv()

    for part, buf in zip(parts, moms):
        part.gather_end(buf)

    def wide(q, value):
        return value[:, columns(q)]

    @pl.loop(0, NZ * NY)
    def _(t):
        zz = t // NY
        yy = lax.rem(t, NY)
        for xx in range(NX):
            rows = pl.ds(pl.multiple_of((t * NX + xx) * OWN, OWN), OWN)
            uu, vv = mixed(xx, yy), mixed(yy, xx)
            gradient = (own_g[rows, :] + peer_rx[rows, :].astype(F32)) * factor
            base = gradient + werr_v[rows, :].astype(F32)
            before = [mom[0, xx, yy, zz], mom[1, yy, xx, zz], mom[2, uu, vv, zz], mom_c[zz, yy, xx]]
            combined = [
                beta_one * before[q].astype(F32) + wide(q, base) for q in range(4)
            ]
            size = jnp.abs(combined[0]) + jnp.abs(combined[1])
            size += jnp.abs(combined[2]) + jnp.abs(combined[3])
            scale = jnp.sum(size, axis=1, keepdims=True) * (1.0 / WIDTH) + tiny_scale
            inverse = 1.0 / scale
            for q in range(4):
                codes = jnp.clip(combined[q] * inverse, -1.0, 1.0).astype(BF16)
                decoded = codes.astype(F32) * scale
                left_v[rows, columns(q)] = (combined[q] - decoded).astype(BF16)
                sent = decoded.astype(BF16)
                if q == 0:
                    dec[0, xx, yy, zz] = sent
                elif q == 1:
                    dec[1, yy, xx, zz] = sent
                elif q == 2:
                    dec[2, uu, vv, zz] = sent
                else:
                    dec_c[zz, yy, xx] = sent

    store_left = pltpu.make_async_copy(left_v, left_out, out_sems.at[0])
    store_left.start()

    decs, gots = bufs(dec, dec_c), bufs(got, got_c)
    halves, mids = bufs(partial, partial_c), bufs(got_mid, got_mid_c)
    totals, firsts = bufs(sums, sums_c), bufs(got_first, got_first_c)
    for part, d, g in zip(parts, decs, gots):
        part.reduce_last(d, g)
    for hop in (2, 3, 4):
        for part, d in zip(parts, decs):
            part.reduce_last_relay(d, hop)
    order = [1, 2, 3, 0]
    for i in order:
        parts[i].reduce_mid(decs[i], gots[i], halves[i], mids[i])
    for i in order:
        parts[i].reduce_mid_relay()
    for i in order:
        parts[i].reduce_first(halves[i], mids[i], totals[i], firsts[i])
    summed = [None] * 4
    for i in order:
        summed[quarter[i]] = parts[i].reduce_end(totals[i], firsts[i])

    load_serr.wait()
    load_master.wait()
    load_variance.wait()
    shifted = [summed[q] * (1.0 / (NX * NY * NZ)) + serr_v[:, columns(q)] for q in range(4)]
    size = jnp.abs(shifted[0]) + jnp.abs(shifted[1])
    size += jnp.abs(shifted[2]) + jnp.abs(shifted[3])
    scale = jnp.sum(size, axis=1, keepdims=True) * (1.0 / WIDTH) + tiny_scale
    wts_all = bufs(wts, wts_c)
    for i, part in enumerate(parts):
        q = quarter[i]
        codes = jnp.clip(shifted[q] / scale, -1.0, 1.0).astype(BF16)
        codes_v[:, columns(q)] = codes
        momentum = codes.astype(F32) * scale
        server_v[:, columns(q)] = shifted[q] - momentum
        new = master_v[:, columns(q)] - learn_rate * momentum / (
            jnp.sqrt(variance_v[:, columns(q)]) + tiny_root
        )
        new_master_v[:, columns(q)] = new
        wts_all[i][part.last, part.mid, part.first] = new.astype(BF16)
        part.gather_first(wts_all[i])
    scale_out[...] = jnp.sum(
        jnp.where(eye, jnp.broadcast_to(scale, (OWN, OWN)), 0.0), axis=0, keepdims=True
    )
    stores = [
        pltpu.make_async_copy(codes_v, codes_out, out_sems.at[1]),
        pltpu.make_async_copy(server_v, server_out, out_sems.at[2]),
        pltpu.make_async_copy(new_master_v, master_out, out_sems.at[3]),
    ]
    for copy in stores:
        copy.start()

    for part, buf in zip(parts, wts_all):
        part.gather_mid(buf)
    for part, buf in zip(parts, wts_all):
        part.gather_mid_relay(buf)
    for part, buf in zip(parts, wts_all):
        part.gather_last(buf)
    for hop in (2, 3, 4):
        for part, buf in zip(parts, wts_all):
            part.gather_last_relay(buf, hop)
    for i in order:
        parts[i].gather_end(wts_all[i])

    def place(k):
        xx, yy = lax.rem(k, NX), k // NX
        return [
            pltpu.make_async_copy(
                src, weights_out.at[:, yy, xx, :, pl.ds(q * LANES, LANES)], out_sems.at[4 + k * 3 + q]
            )
            for q, src in enumerate(
                [wts.at[0, xx, yy], wts.at[1, yy, xx], wts.at[2, mixed(xx, yy), mixed(yy, xx)]]
            )
        ]

    @pl.loop(0, NX * NY)
    def _(k):
        for copy in place(k):
            copy.start()

    whole = pltpu.make_async_copy(
        wts_c, weights_out.at[:, :, :, :, pl.ds(3 * LANES, LANES)], out_sems.at[4 + 3 * NX * NY]
    )
    whole.start()

    @pl.loop(0, NX * NY)
    def _(k):
        for copy in place(k):
            copy.wait()

    whole.wait()
    store_left.wait()
    for copy in stores:
        copy.wait()
    assert links.used == REMOTE_COPIES
    links.drain()

    @pl.loop(0, CHUNKS)
    def _(k):
        peer_copy(k).wait_send()


REMOTE_COPIES = 288


def body(act, grads, werr, mcodes, mscale, serr, master, variance):
    tokens = act.shape[0]
    any_spec = pl.BlockSpec(memory_space=pl.ANY)
    vmem_spec = pl.BlockSpec(memory_space=pltpu.VMEM)
    tile = (OWN, LANES)

    def vm(*shape, dtype=BF16):
        return pltpu.VMEM(shape, dtype)

    scratch = [
        vm(2 * CHUNKS, tokens, CHUNK),
        vm(tokens, WIDTH),
        vm(HALF, WIDTH),
        vm(OWN, WIDTH),
        vm(OWN, WIDTH, dtype=F32),
        vm(OWN, WIDTH, dtype=F32),
        vm(OWN, WIDTH, dtype=F32),
        vm(HALF, WIDTH),
        vm(OWN, WIDTH),
        vm(OWN, WIDTH, dtype=F32),
        vm(OWN, WIDTH, dtype=F32),
        vm(HALF, WIDTH, dtype=F32),
        vm(HALF, WIDTH),
        vm(HALF, WIDTH),
    ]
    for _ in range(3):
        scratch += [vm(3, 4, 4, NZ, *tile), vm(NZ, 4, 4, *tile)]
    scratch += [
        vm(3, 2, 2, 4, NZ, *tile),
        vm(2, 4, 4, 4, *tile),
        vm(3, 4, NZ, *tile),
        vm(4, 4, *tile),
        vm(3, 2, 2, NZ, *tile),
        vm(2, 2, 4, *tile),
        vm(3, NZ, *tile, dtype=F32),
        vm(4, *tile, dtype=F32),
        vm(3, NZ - 1, *tile, dtype=F32),
        vm(3, *tile, dtype=F32),
    ]
    dma = pltpu.SemaphoreType.DMA
    scratch += [
        dma((6,)),
        dma((2 * CHUNKS,)),
        dma((5 + 3 * NX * NY,)),
        dma((CHUNKS,)),
        dma((CHUNKS,)),
        dma((REMOTE_COPIES,)),
        dma((REMOTE_COPIES,)),
    ]
    shape = jax.ShapeDtypeStruct
    left, codes, scale, server, new_master, weights = pl.pallas_call(
        step_kernel,
        out_shape=[
            shape((HALF, WIDTH), BF16),
            shape((OWN, WIDTH), BF16),
            shape((1, OWN), F32),
            shape((OWN, WIDTH), F32),
            shape((OWN, WIDTH), F32),
            shape((NZ, NY, NX, OWN, WIDTH), BF16),
        ],
        in_specs=[any_spec] * 4 + [vmem_spec] + [any_spec] * 3,
        out_specs=[any_spec, any_spec, vmem_spec, any_spec, any_spec, any_spec],
        scratch_shapes=scratch,
        compiler_params=pltpu.CompilerParams(
            collective_id=0, has_side_effects=True, vmem_limit_bytes=48 * 1024 * 1024
        ),
        cost_estimate=pl.CostEstimate(
            flops=2 * tokens * 2 * HALF * WIDTH, bytes_accessed=14_000_000, transcendentals=0
        ),
        name="adam_step",
    )(act, grads, werr[0], mcodes, mscale.reshape(1, OWN), serr, master, variance)
    return (
        left[None],
        codes,
        scale.reshape(OWN),
        server,
        new_master,
        weights.reshape(HALF, WIDTH),
    )


def solution(mesh):
    return jax.shard_map(
        body,
        mesh=mesh,
        in_specs=(
            P(("dp", "rep"), None),
            P(("dp", "rep"), None),
            P("dp", "rep", None),
            P(("rep", "dp"), None),
            P(("rep", "dp")),
            P(("rep", "dp"), None),
            P(("rep", "dp"), None),
            P(("rep", "dp"), None),
        ),
        out_specs=(
            P("dp", "rep", None),
            P(("rep", "dp"), None),
            P(("rep", "dp")),
            P(("rep", "dp"), None),
            P(("rep", "dp"), None),
            P("rep", None),
        ),
        check_vma=False,
    )
```

```python
import functools
import math

import jax
import jax.numpy as jnp
from jax import lax
from jax.experimental import pallas as pl
from jax.experimental.pallas import tpu as pltpu
from jax.sharding import PartitionSpec as P

BF16 = jnp.bfloat16
F32 = jnp.float32
MESH = pl.DeviceIdType.MESH

NX, NY, NZ = 4, 4, 8
RING = 4
OWN = 16
PART = 256
CHUNK = 256
HALF = 2048
WIDTH = 512
CHUNKS = HALF // CHUNK

beta_one = 0.9
learn_rate = 0.02
grad_boost = 8.0
tiny_scale = 1e-06
tiny_root = 1e-08


class Part:
    def __init__(self, column, p, q, dp_pq, core, send_sems, recv_sems):
        self.columns = slice(column, column + PART)
        self.p, self.q, self.dp_pq, self.core = p, q, dp_pq, core
        self.send_sems, self.recv_sems = send_sems, recv_sems

    def at_p(self, k):
        return lax.rem(self.p + (k + RING), RING)

    def at_q(self, k):
        return lax.rem(self.q + (k + RING), RING)

    def shard(self, buf, p, q, z):
        return buf.at[(p * RING + q) * NZ + z]

    def block(self, buf, p, q):
        return buf.at[pl.ds((p * RING + q) * NZ, NZ)]

    def half(self, buf, p, q, which):
        return buf.at[pl.ds((p * RING + q) * NZ + which * (NZ // 2), NZ // 2)]

    def send(self, src, dst, send, recv, dp):
        pltpu.make_async_remote_copy(
            src_ref=src,
            dst_ref=dst,
            send_sem=self.send_sems.at[send],
            recv_sem=self.recv_sems.at[recv],
            device_id={"dp": dp, "rep": self.core},
            device_id_type=MESH,
        ).start()

    def wait(self, like, recv):
        pltpu.make_async_copy(like, like, self.recv_sems.at[recv]).wait()

    def drain(self, like, send):
        pltpu.make_async_copy(like, like, self.send_sems.at[send]).wait()


G_FIRST, G_MID, G_LEFT, G_RIGHT, G_REST, G_COUNT = 0, 0, 4, 8, 12, 16
R_FIRST, R_MID, R_LEFT, R_RIGHT, R_REST, R_COUNT = 0, 1, 2, 6, 10, 14
G_SENDS, R_SENDS = 0, 1


class Gather:
    def __init__(self, part, buf, z, send, recv):
        self.part, self.buf, self.z, self.send_sem, self.recv = part, buf, z, send, recv

    def go(self, src, dst_recv, dp):
        self.part.send(src, src, self.send_sem, self.recv + dst_recv, dp)

    def first(self, dp_z):
        mine = self.part.shard(self.buf, self.part.p, self.part.q, self.z)
        for k in range(1, NZ):
            self.go(mine, G_FIRST, dp_z(lax.rem(self.z + k, NZ)))

    def first_here(self):
        self.part.wait(self.buf.at[pl.ds(0, NZ - 1)], self.recv + G_FIRST)

    def mid(self):
        part = self.part
        for k in (1, 3, 2):
            self.go(part.block(self.buf, part.p, part.q), G_MID + k, part.dp_pq(part.p, part.at_q(k)))

    def mid_here(self, k):
        part = self.part
        part.wait(part.block(self.buf, part.p, part.at_q(-k)), self.recv + G_MID + k)

    def last(self, row):
        part = self.part
        q = part.at_q(row)
        lower, upper = part.half(self.buf, part.p, q, 0), part.half(self.buf, part.p, q, 1)
        after = part.dp_pq(part.at_p(1), part.q)
        before = part.dp_pq(part.at_p(-1), part.q)
        self.go(lower, G_LEFT + row, after)
        self.go(upper, G_RIGHT + row, before)
        self.go(upper, G_REST + row, after)
        self.go(lower, G_REST + row, before)

    def relay(self, row):
        part = self.part
        q = part.at_q(row)
        lower = part.half(self.buf, part.at_p(-1), q, 0)
        part.wait(lower, self.recv + G_LEFT + row)
        self.go(lower, G_REST + row, part.dp_pq(part.at_p(1), part.q))
        upper = part.half(self.buf, part.at_p(1), q, 1)
        part.wait(upper, self.recv + G_RIGHT + row)
        self.go(upper, G_REST + row, part.dp_pq(part.at_p(-1), part.q))

    def row_here(self, row):
        self.part.wait(self.buf.at[pl.ds(0, 2 * NZ)], self.recv + G_REST + row)

    def drain(self):
        self.part.drain(self.buf.at[pl.ds(0, NX * NY * NZ - 1)], self.send_sem)


def gather_rest(gathers, before_blocks, own_block, near_rows, all_rows):
    for g in gathers:
        g.first_here()
    for g in gathers:
        g.mid()
        g.last(0)
    before_blocks()
    for k in (1, 3):
        for g in gathers:
            g.mid_here(k)
            g.last(RING - k)
    for g in gathers:
        g.relay(0)
    for g in gathers:
        g.mid_here(2)
        g.last(2)
    own_block()
    for row in (3, 1):
        for g in gathers:
            g.relay(row)
    for row in (0, 3, 1):
        for g in gathers:
            g.row_here(row)
    near_rows()
    for g in gathers:
        g.relay(2)
    for g in gathers:
        g.row_here(2)
    all_rows()


class Reduce:
    def __init__(self, part, dec, z, send, recv, near, far, partial, mids, sums, rounded, firsts):
        self.part, self.dec, self.z, self.send_sem, self.recv = part, dec, z, send, recv
        self.near, self.far, self.partial = near, far, partial
        self.mids, self.sums, self.rounded, self.firsts = mids, sums, rounded, firsts

    def go(self, src, dst, recv, dp):
        self.part.send(src, dst, self.send_sem, self.recv + recv, dp)

    def steps(self, row):
        part = self.part
        return (
            part.at_q(row),
            part.dp_pq(part.at_p(1), part.q),
            part.dp_pq(part.at_p(-1), part.q),
        )

    def half_of(self, row, way, which):
        return self.far.at[row, pl.ds(way * NZ + which * (NZ // 2), NZ // 2)]

    def last_far(self, row):
        part = self.part
        q, after, before = self.steps(row)
        opposite = part.at_p(2)
        self.go(part.half(self.dec, opposite, q, 0), self.near.at[row, 0], R_LEFT + row, after)
        self.go(part.half(self.dec, opposite, q, 1), self.near.at[row, 1], R_RIGHT + row, before)

    def last_own(self, row):
        part = self.part
        q, after, before = self.steps(row)
        self.go(part.half(self.dec, part.at_p(1), q, 1), self.half_of(row, 0, 1), R_REST + row, after)
        self.go(part.half(self.dec, part.at_p(-1), q, 0), self.half_of(row, 1, 0), R_REST + row, before)

    def last_relay(self, row):
        part = self.part
        q, after, before = self.steps(row)
        for way, sem, to, dp in ((0, R_LEFT, 1, after), (1, R_RIGHT, -1, before)):
            got = self.near.at[row, way]
            part.wait(got, self.recv + sem + row)
            mine = part.half(self.dec, part.at_p(to), q, way)
            mine[...] = (mine[...].astype(F32) + got[...].astype(F32)).astype(BF16)
            self.go(mine, self.half_of(row, way, way), R_REST + row, dp)

    def row_total(self, row):
        part = self.part
        part.wait(self.far.at[row], self.recv + R_REST + row)
        total = part.block(self.dec, part.p, part.at_q(row))[...].astype(F32)
        return total + (
            self.far[row, pl.ds(0, NZ)].astype(F32) + self.far[row, pl.ds(NZ, NZ)].astype(F32)
        )

    def mid(self, row):
        part = self.part
        self.partial[row] = self.row_total(row).astype(BF16)
        self.go(
            self.partial.at[row],
            self.mids.at[pl.ds((row - 1) * NZ, NZ)],
            R_MID,
            part.dp_pq(part.p, part.at_q(row)),
        )

    def mid_own(self):
        self.sums[...] = self.row_total(0)

    def first(self, dp_z):
        self.part.wait(self.mids, self.recv + R_MID)
        total = self.sums[...]
        for k in range(RING - 1):
            total += self.mids[pl.ds(k * NZ, NZ)].astype(F32)
        self.sums[...] = total
        self.rounded[...] = total.astype(BF16)
        for k in range(1, NZ):
            to = lax.rem(self.z + k, NZ)
            self.go(self.rounded.at[to], self.firsts.at[k - 1], R_FIRST, dp_z(to))

    def total(self):
        self.part.wait(self.firsts, self.recv + R_FIRST)
        total = self.sums[self.z]
        for k in range(NZ - 1):
            total += self.firsts[k].astype(F32)
        return total

    def drain(self):
        self.part.drain(self.dec.at[pl.ds(0, NX * NY * NZ - 1)], self.send_sem)


def step_kernel(
    act, grads, werr, mcodes, mscale, serr, master, variance,
    left_out, codes_out, scale_out, server_out, master_out, weights_out,
    act_v, grads_v, werr_v, mcodes_v, serr_v, master_v, variance_v,
    left_v, codes_v, server_v, new_master_v,
    own_g, peer_tx, peer_rx,
    mom, dec, wts, near, far, partial, mids, sums, rounded, firsts,
    in_sems, act_sems, out_sems, peer_send, peer_recv, send_sems, recv_sems,
):
    dp = lax.axis_index("dp")
    core = lax.axis_index("rep")
    x = lax.rem(dp, NX)
    y = lax.rem(dp // NX, NY)
    z = dp // (NX * NY)
    other = 1 - core
    tokens = act.shape[0]
    factor = (1.0 - beta_one) * grad_boost / math.sqrt(2 * tokens)

    def load(k, src, dst):
        copy = pltpu.make_async_copy(src, dst, in_sems.at[k])
        copy.start()
        return copy

    load_codes = load(0, mcodes, mcodes_v)

    def dp_at(zz, yy, xx):
        return zz * (NX * NY) + yy * NX + xx

    def dp_z(zz):
        return dp_at(zz, y, x)

    barrier = pltpu.get_barrier_semaphore()
    peers = [(dp_at(lax.rem(z + k, NZ), y, x), core) for k in range(1, NZ)]
    peers += [(dp_at(z, y, lax.rem(x + k, NX)), core) for k in range(1, NX)]
    peers += [(dp_at(z, lax.rem(y + k, NY), x), core) for k in range(1, NY)]
    peers += [(dp, other)]
    for peer_dp, peer_core in peers:
        pl.semaphore_signal(
            barrier, inc=1, device_id={"dp": peer_dp, "rep": peer_core}, device_id_type=MESH
        )

    load_grads = load(1, grads, grads_v)

    def act_copy(k):
        base = jnp.where(k < CHUNKS, other * HALF, core * HALF)
        column = pl.multiple_of(base + lax.rem(k, CHUNKS) * CHUNK, CHUNK)
        return pltpu.make_async_copy(
            act.at[:, pl.ds(column, CHUNK)], act_v.at[k], act_sems.at[k]
        )

    @pl.loop(0, 2 * CHUNKS)
    def _(k):
        act_copy(k).start()

    load_werr = load(2, werr, werr_v)
    load_serr = load(3, serr, serr_v)
    load_master = load(4, master, master_v)
    load_variance = load(5, variance, variance_v)

    eye = lax.broadcasted_iota(jnp.int32, (OWN, OWN), 0) == lax.broadcasted_iota(
        jnp.int32, (OWN, OWN), 1
    )
    scale_col = jnp.sum(
        jnp.where(eye, jnp.broadcast_to(mscale[...], (OWN, OWN)), 0.0), axis=1, keepdims=True
    )
    load_codes.wait()
    previous = (mcodes_v[...].astype(F32) * scale_col).astype(BF16)

    parts = [
        Part(0, x, y, lambda p, q: dp_at(z, q, p), core, send_sems, recv_sems),
        Part(PART, y, x, lambda p, q: dp_at(z, p, q), core, send_sems, recv_sems),
    ]
    gathers = []
    for i, part in enumerate(parts):
        part.shard(mom.at[i], part.p, part.q, z)[...] = previous[:, part.columns]
        gathers.append(Gather(part, mom.at[i], z, 3 * i, i * G_COUNT))
    pl.semaphore_wait(barrier, len(peers))
    for g in gathers:
        g.first(dp_z)

    def product(k):
        act_copy(k).wait()
        return lax.dot_general(
            act_v[k], grads_v[...], (((0,), (0,)), ((), ())), preferred_element_type=F32
        )

    def chunk_rows(k):
        return pl.ds(pl.multiple_of(k * CHUNK, CHUNK), CHUNK)

    def peer_copy(k):
        rows = chunk_rows(k)
        return pltpu.make_async_remote_copy(
            src_ref=peer_tx.at[rows],
            dst_ref=peer_rx.at[rows],
            send_sem=peer_send.at[0],
            recv_sem=peer_recv.at[0],
            device_id={"dp": dp, "rep": other},
            device_id_type=MESH,
        )

    load_grads.wait()

    @pl.loop(0, CHUNKS)
    def _(k):
        peer_tx[chunk_rows(k)] = product(k).astype(BF16)
        peer_copy(k).start()

    def for_own(lo, hi):
        @pl.loop(lo, hi)
        def _(k):
            own_g[chunk_rows(k)] = product(k + CHUNKS)

    for_own(0, 4)

    def compress(lo, hi, place):
        @pl.loop(lo * 2, hi * 2)
        def _(t):
            dx, dy = place(t // 2)
            xx, yy = lax.rem(x + dx, NX), lax.rem(y + dy, NY)
            for k in range(NZ // 2):
                zz = lax.rem(t, 2) * (NZ // 2) + k
                rows = pl.ds(pl.multiple_of(dp_at(zz, yy, xx) * OWN, OWN), OWN)
                at = [(xx * RING + yy) * NZ + zz, (yy * RING + xx) * NZ + zz]
                gradient = (own_g[rows, :] + peer_rx[rows, :].astype(F32)) * factor
                base = gradient + werr_v[rows, :].astype(F32)
                combined = [
                    beta_one * mom[i, at[i]].astype(F32) + base[:, part.columns]
                    for i, part in enumerate(parts)
                ]
                size = jnp.abs(combined[0]) + jnp.abs(combined[1])
                scale = jnp.sum(size, axis=1, keepdims=True) * (1.0 / WIDTH) + tiny_scale
                inverse = 1.0 / scale
                for i, part in enumerate(parts):
                    codes = jnp.clip(combined[i] * inverse, -1.0, 1.0).astype(BF16)
                    decoded = codes.astype(F32) * scale
                    left_v[rows, part.columns] = (combined[i] - decoded).astype(BF16)
                    dec[i, at[i]] = decoded.astype(BF16)

    def skip_two(k):
        return k + k // 2

    def finish_gradient():
        for_own(4, 8)
        load_werr.wait()
        pltpu.make_async_copy(peer_rx, peer_rx, peer_recv.at[0]).wait()

    def compress_own():
        compress(0, 1, lambda t: (0, 0))

    def compress_near():
        compress(1, 9, lambda t: (skip_two(t // 3), skip_two(lax.rem(t, 3))))

    def compress_far():
        compress(0, 4, lambda t: (2, t))
        compress(0, 3, lambda t: (skip_two(t), 2))

    gather_rest(gathers, finish_gradient, compress_own, compress_near, compress_far)

    reduces = [
        Reduce(
            part, dec.at[i], z, 3 * i + 1, 4 * G_COUNT + i * R_COUNT, near.at[i], far.at[i],
            partial.at[i], mids.at[i], sums.at[i], rounded.at[i], firsts.at[i],
        )
        for i, part in enumerate(parts)
    ]
    rows = (1, 2, 3, 0)
    for row in rows:
        for r in reduces:
            r.last_far(row)
    for row in rows:
        for r in reduces:
            r.last_own(row)
    store_left = pltpu.make_async_copy(left_v, left_out, out_sems.at[0])
    store_left.start()

    @pl.loop(0, RING)
    def _(t):
        for r in reduces:
            r.last_relay(lax.rem(t + 1, RING))

    @pl.loop(1, RING)
    def _(row):
        for r in reduces:
            r.mid(row)

    for r in reduces:
        r.mid_own()
    for r in reduces:
        r.first(dp_z)
    load_serr.wait()
    load_master.wait()
    load_variance.wait()
    summed = [r.total() for r in reduces]

    shifted = [
        summed[i] * (1.0 / (NX * NY * NZ)) + serr_v[:, part.columns]
        for i, part in enumerate(parts)
    ]
    size = jnp.abs(shifted[0]) + jnp.abs(shifted[1])
    scale = jnp.sum(size, axis=1, keepdims=True) * (1.0 / WIDTH) + tiny_scale
    gathers_w = []
    for i, part in enumerate(parts):
        codes = jnp.clip(shifted[i] / scale, -1.0, 1.0).astype(BF16)
        codes_v[:, part.columns] = codes
        momentum = codes.astype(F32) * scale
        server_v[:, part.columns] = shifted[i] - momentum
        new = master_v[:, part.columns] - learn_rate * momentum / (
            jnp.sqrt(variance_v[:, part.columns]) + tiny_root
        )
        new_master_v[:, part.columns] = new
        part.shard(wts.at[i], part.p, part.q, z)[...] = new.astype(BF16)
        g = Gather(part, wts.at[i], z, 3 * i + 2, (2 + i) * G_COUNT)
        g.first(dp_z)
        gathers_w.append(g)
    scale_out[...] = jnp.sum(
        jnp.where(eye, jnp.broadcast_to(scale, (OWN, OWN)), 0.0), axis=0, keepdims=True
    )
    stores = [
        store_left,
        pltpu.make_async_copy(codes_v, codes_out, out_sems.at[1]),
        pltpu.make_async_copy(server_v, server_out, out_sems.at[2]),
        pltpu.make_async_copy(new_master_v, master_out, out_sems.at[3]),
    ]
    for copy in stores[1:]:
        copy.start()

    def place(row):
        for i, g in enumerate(gathers_w):
            q = g.part.at_q(row)
            for p in range(RING):
                xx, yy = (p, q) if i == 0 else (q, p)
                pltpu.make_async_copy(
                    g.part.block(g.buf, p, q),
                    weights_out.at[:, yy, xx, :, pl.ds(i * PART, PART)],
                    out_sems.at[4],
                ).start()

    def place_near():
        for row in (0, 3, 1):
            place(row)

    gather_rest(gathers_w, lambda: None, lambda: None, place_near, lambda: place(2))
    pltpu.make_async_copy(weights_out, weights_out, out_sems.at[4]).wait()
    for copy in stores:
        copy.wait()
    for g in gathers + gathers_w + reduces:
        g.drain()
    pltpu.make_async_copy(peer_tx, peer_tx, peer_send.at[0]).wait()


def copy_kernel(count, *refs):
    sources, targets, rooms = refs[:count], refs[count : 2 * count], refs[2 * count : 3 * count]
    sems = refs[-1]
    pieces = []
    for i in range(count):
        rows = sources[i].shape[0]
        step = max(rows // 8, 1) if rows > OWN else rows
        pieces += [(i, k, step) for k in range(0, rows, step)]

    def copies(n):
        i, k, step = pieces[n]
        at = pl.ds(k, step)
        return (
            pltpu.make_async_copy(sources[i].at[at], rooms[i].at[at], sems.at[0, n]),
            pltpu.make_async_copy(rooms[i].at[at], targets[i].at[at], sems.at[1, n]),
        )

    for n in range(len(pieces)):
        copies(n)[0].start()
    for n in range(len(pieces)):
        copies(n)[0].wait()
        copies(n)[1].start()
    for n in range(len(pieces)):
        copies(n)[1].wait()


def copied(arrays):
    spec = pl.BlockSpec(memory_space=pltpu.HBM)
    return pl.pallas_call(
        functools.partial(copy_kernel, len(arrays)),
        out_shape=[jax.ShapeDtypeStruct(a.shape, a.dtype) for a in arrays],
        in_specs=[spec] * len(arrays),
        out_specs=[spec] * len(arrays),
        scratch_shapes=[pltpu.VMEM(a.shape, a.dtype) for a in arrays]
        + [pltpu.SemaphoreType.DMA((2, 20))],
        compiler_params=pltpu.CompilerParams(vmem_limit_bytes=56 * 1024 * 1024),
        name="hand_out",
    )(*arrays)


def body(act, grads, werr, mcodes, mscale, serr, master, variance):
    tokens = act.shape[0]
    hbm = pl.BlockSpec(memory_space=pltpu.HBM)
    vmem = pl.BlockSpec(memory_space=pltpu.VMEM)
    shards = NX * NY * NZ
    tile = (OWN, PART)

    def vm(*shape, dtype=BF16):
        return pltpu.VMEM(shape, dtype)

    scratch = [
        vm(2 * CHUNKS, tokens, CHUNK),
        vm(tokens, WIDTH),
        vm(HALF, WIDTH),
        vm(OWN, WIDTH),
        vm(OWN, WIDTH, dtype=F32),
        vm(OWN, WIDTH, dtype=F32),
        vm(OWN, WIDTH, dtype=F32),
        vm(HALF, WIDTH),
        vm(OWN, WIDTH),
        vm(OWN, WIDTH, dtype=F32),
        vm(OWN, WIDTH, dtype=F32),
        vm(HALF, WIDTH, dtype=F32),
        vm(HALF, WIDTH),
        vm(HALF, WIDTH),
        vm(2, shards, *tile),
        vm(2, shards, *tile),
        vm(2, shards, *tile),
        vm(2, RING, 2, NZ // 2, *tile),
        vm(2, RING, 2 * NZ, *tile),
        vm(2, RING, NZ, *tile),
        vm(2, (RING - 1) * NZ, *tile),
        vm(2, NZ, *tile, dtype=F32),
        vm(2, NZ, *tile),
        vm(2, NZ - 1, *tile),
    ]
    dma = pltpu.SemaphoreType.DMA
    scratch += [
        dma((6,)),
        dma((2 * CHUNKS,)),
        dma((5,)),
        dma((1,)),
        dma((1,)),
        dma((6,)),
        dma((4 * G_COUNT + 2 * R_COUNT,)),
    ]
    shape = jax.ShapeDtypeStruct
    outs = pl.pallas_call(
        step_kernel,
        out_shape=[
            shape((HALF, WIDTH), BF16),
            shape((OWN, WIDTH), BF16),
            shape((1, OWN), F32),
            shape((OWN, WIDTH), F32),
            shape((OWN, WIDTH), F32),
            shape((NZ, NY, NX, OWN, WIDTH), BF16),
        ],
        in_specs=[hbm] * 4 + [vmem] + [hbm] * 3,
        out_specs=[hbm, hbm, vmem, hbm, hbm, hbm],
        scratch_shapes=scratch,
        compiler_params=pltpu.CompilerParams(
            collective_id=0, has_side_effects=True, vmem_limit_bytes=56 * 1024 * 1024
        ),
        cost_estimate=pl.CostEstimate(
            flops=2 * tokens * 2 * HALF * WIDTH, bytes_accessed=14_000_000, transcendentals=0
        ),
        name="adam_step",
    )(act, grads, werr[0], mcodes, mscale.reshape(1, OWN), serr, master, variance)
    outs = [*outs[:-1], outs[-1].reshape(HALF, WIDTH)]
    left, codes, scale, server, new_master, weights = copied(outs)
    return (
        left[None],
        codes,
        scale.reshape(OWN),
        server,
        new_master,
        weights,
    )


def solution(mesh):
    return jax.shard_map(
        body,
        mesh=mesh,
        in_specs=(
            P(("dp", "rep"), None),
            P(("dp", "rep"), None),
            P("dp", "rep", None),
            P(("rep", "dp"), None),
            P(("rep", "dp")),
            P(("rep", "dp"), None),
            P(("rep", "dp"), None),
            P(("rep", "dp"), None),
        ),
        out_specs=(
            P("dp", "rep", None),
            P(("rep", "dp"), None),
            P(("rep", "dp")),
            P(("rep", "dp"), None),
            P(("rep", "dp"), None),
            P("rep", None),
        ),
        check_vma=False,
    )
```

```python
import functools
import math

import jax
import jax.numpy as jnp
from jax import lax
from jax.experimental import pallas as pl
from jax.experimental.pallas import tpu as pltpu
from jax.sharding import PartitionSpec as P

BF16 = jnp.bfloat16
F32 = jnp.float32
MESH = pl.DeviceIdType.MESH

NX, NY, NZ = 4, 4, 8
RING = 4
OWN = 16
PART = 256
CHUNK = 256
HALF = 2048
WIDTH = 512
CHUNKS = HALF // CHUNK

beta_one = 0.9
learn_rate = 0.02
grad_boost = 8.0
tiny_scale = 1e-06
tiny_root = 1e-08


class Part:
    def __init__(self, column, p, q, dp_pq, core, send_sems, recv_sems):
        self.columns = slice(column, column + PART)
        self.p, self.q, self.dp_pq, self.core = p, q, dp_pq, core
        self.send_sems, self.recv_sems = send_sems, recv_sems

    def at_p(self, k):
        return lax.rem(self.p + (k + RING), RING)

    def at_q(self, k):
        return lax.rem(self.q + (k + RING), RING)

    def shard(self, buf, p, q, z):
        return buf.at[(p * RING + q) * NZ + z]

    def block(self, buf, p, q):
        return buf.at[pl.ds((p * RING + q) * NZ, NZ)]

    def half(self, buf, p, q, which):
        return buf.at[pl.ds((p * RING + q) * NZ + which * (NZ // 2), NZ // 2)]

    def send(self, src, dst, send, recv, dp):
        pltpu.make_async_remote_copy(
            src_ref=src,
            dst_ref=dst,
            send_sem=self.send_sems.at[send],
            recv_sem=self.recv_sems.at[recv],
            device_id={"dp": dp, "rep": self.core},
            device_id_type=MESH,
        ).start()

    def wait(self, like, recv):
        pltpu.make_async_copy(like, like, self.recv_sems.at[recv]).wait()

    def drain(self, like, send):
        pltpu.make_async_copy(like, like, self.send_sems.at[send]).wait()


G_FIRST, G_MID, G_ROW, G_COUNT = 0, 0, 4, 8
R_FIRST, R_MID, R_ROW, R_COUNT = 0, 1, 2, 6


class Gather:
    def __init__(self, part, buf, z, send, recv):
        self.part, self.buf, self.z, self.send_sem, self.recv = part, buf, z, send, recv

    def go(self, src, dst_recv, dp):
        self.part.send(src, src, self.send_sem, self.recv + dst_recv, dp)

    def first(self, dp_z):
        mine = self.part.shard(self.buf, self.part.p, self.part.q, self.z)
        for k in (4, 3, 5, 2, 6, 1, 7):
            self.go(mine, G_FIRST, dp_z(lax.rem(self.z + k, NZ)))

    def first_here(self):
        self.part.wait(self.buf.at[pl.ds(0, NZ - 1)], self.recv + G_FIRST)

    def mid(self):
        part = self.part
        for k in (2, 1, 3):
            self.go(part.block(self.buf, part.p, part.q), G_MID + k, part.dp_pq(part.p, part.at_q(k)))

    def mid_here(self, k):
        part = self.part
        part.wait(part.block(self.buf, part.p, part.at_q(-k)), self.recv + G_MID + k)

    def last(self, row):
        part = self.part
        block = part.block(self.buf, part.p, part.at_q(row))
        for k in (2, 1, 3):
            self.go(block, G_ROW + row, part.dp_pq(part.at_p(k), part.q))

    def row_here(self, row):
        self.part.wait(self.buf.at[pl.ds(0, 3 * NZ)], self.recv + G_ROW + row)

    def drain(self):
        self.part.drain(self.buf.at[pl.ds(0, NX * NY * NZ - 1)], self.send_sem)


def gather_rest(gathers, first_sent, own_block, near_rows, all_rows):
    for g in gathers:
        g.first_here()
    for g in gathers:
        g.mid()
        g.last(0)
    first_sent()
    for k in (1, 3):
        for g in gathers:
            g.mid_here(k)
            g.last(RING - k)
    for g in gathers:
        g.mid_here(2)
        g.last(2)
    own_block()
    for row in (0, 3, 1):
        for g in gathers:
            g.row_here(row)
    near_rows()
    for g in gathers:
        g.row_here(2)
    all_rows()


class Reduce:
    def __init__(self, part, dec, z, send, recv, far, partial, mids, sums, rounded, firsts):
        self.part, self.dec, self.z, self.send_sem, self.recv = part, dec, z, send, recv
        self.far, self.partial = far, partial
        self.mids, self.sums, self.rounded, self.firsts = mids, sums, rounded, firsts

    def go(self, src, dst, recv, dp):
        self.part.send(src, dst, self.send_sem, self.recv + recv, dp)

    def last(self, row, k):
        part = self.part
        self.go(
            part.block(self.dec, part.at_p(k), part.at_q(row)),
            self.far.at[row, pl.ds((k - 1) * NZ, NZ)],
            R_ROW + row,
            part.dp_pq(part.at_p(k), part.q),
        )

    def row_total(self, row):
        part = self.part
        part.wait(self.far.at[row], self.recv + R_ROW + row)
        total = part.block(self.dec, part.p, part.at_q(row))[...].astype(F32)
        for k in range(RING - 1):
            total += self.far[row, pl.ds(k * NZ, NZ)].astype(F32)
        return total

    def mid(self, row):
        part = self.part
        self.partial[row] = self.row_total(row).astype(BF16)
        self.go(
            self.partial.at[row],
            self.mids.at[pl.ds((row - 1) * NZ, NZ)],
            R_MID,
            part.dp_pq(part.p, part.at_q(row)),
        )

    def mid_own(self):
        self.sums[...] = self.row_total(0)

    def first(self, dp_z):
        self.part.wait(self.mids, self.recv + R_MID)
        total = self.sums[...]
        for k in range(RING - 1):
            total += self.mids[pl.ds(k * NZ, NZ)].astype(F32)
        self.sums[...] = total
        self.rounded[...] = total.astype(BF16)
        for k in range(1, NZ):
            to = lax.rem(self.z + k, NZ)
            self.go(self.rounded.at[to], self.firsts.at[k - 1], R_FIRST, dp_z(to))

    def total(self):
        self.part.wait(self.firsts, self.recv + R_FIRST)
        total = self.sums[self.z]
        for k in range(NZ - 1):
            total += self.firsts[k].astype(F32)
        return total

    def drain(self):
        self.part.drain(self.dec.at[pl.ds(0, NX * NY * NZ - 1)], self.send_sem)


def step_kernel(
    act, grads, werr, mcodes, mscale, serr, master, variance,
    left_out, codes_out, scale_out, server_out, master_out, weights_out,
    act_v, grads_v, werr_v, mcodes_v, serr_v, master_v, variance_v,
    left_v, codes_v, server_v, new_master_v,
    own_g, peer_tx, peer_rx,
    mom, dec, wts, far, partial, mids, sums, rounded, firsts,
    in_sems, act_sems, out_sems, peer_send, peer_recv, send_sems, recv_sems,
):
    dp = lax.axis_index("dp")
    core = lax.axis_index("rep")
    x = lax.rem(dp, NX)
    y = lax.rem(dp // NX, NY)
    z = dp // (NX * NY)
    other = 1 - core
    tokens = act.shape[0]
    factor = (1.0 - beta_one) * grad_boost / math.sqrt(2 * tokens)

    def load(k, src, dst):
        copy = pltpu.make_async_copy(src, dst, in_sems.at[k])
        copy.start()
        return copy

    load_codes = load(0, mcodes, mcodes_v)

    def dp_at(zz, yy, xx):
        return zz * (NX * NY) + yy * NX + xx

    def dp_z(zz):
        return dp_at(zz, y, x)

    barrier = pltpu.get_barrier_semaphore()
    peers = [(dp_at(lax.rem(z + k, NZ), y, x), core) for k in range(1, NZ)]
    peers += [(dp_at(z, y, lax.rem(x + k, NX)), core) for k in range(1, NX)]
    peers += [(dp_at(z, lax.rem(y + k, NY), x), core) for k in range(1, NY)]
    peers += [(dp, other)]
    for peer_dp, peer_core in peers:
        pl.semaphore_signal(
            barrier, inc=1, device_id={"dp": peer_dp, "rep": peer_core}, device_id_type=MESH
        )

    load_grads = load(1, grads, grads_v)

    def act_copy(k):
        base = jnp.where(k < CHUNKS, other * HALF, core * HALF)
        column = pl.multiple_of(base + lax.rem(k, CHUNKS) * CHUNK, CHUNK)
        return pltpu.make_async_copy(
            act.at[:, pl.ds(column, CHUNK)], act_v.at[k], act_sems.at[k]
        )

    @pl.loop(0, 2 * CHUNKS)
    def _(k):
        act_copy(k).start()

    load_werr = load(2, werr, werr_v)
    load_serr = load(3, serr, serr_v)
    load_master = load(4, master, master_v)
    load_variance = load(5, variance, variance_v)

    eye = lax.broadcasted_iota(jnp.int32, (OWN, OWN), 0) == lax.broadcasted_iota(
        jnp.int32, (OWN, OWN), 1
    )
    scale_col = jnp.sum(
        jnp.where(eye, jnp.broadcast_to(mscale[...], (OWN, OWN)), 0.0), axis=1, keepdims=True
    )
    load_codes.wait()
    previous = (mcodes_v[...].astype(F32) * (beta_one * scale_col)).astype(BF16)

    parts = [
        Part(0, x, y, lambda p, q: dp_at(z, q, p), core, send_sems, recv_sems),
        Part(PART, y, x, lambda p, q: dp_at(z, p, q), core, send_sems, recv_sems),
    ]
    gathers = []
    for i, part in enumerate(parts):
        part.shard(mom.at[i], part.p, part.q, z)[...] = previous[:, part.columns]
        gathers.append(Gather(part, mom.at[i], z, 3 * i, i * G_COUNT))
    pl.semaphore_wait(barrier, len(peers))
    for g in gathers:
        g.first(dp_z)

    def product(k):
        act_copy(k).wait()
        return lax.dot_general(
            act_v[k], grads_v[...], (((0,), (0,)), ((), ())), preferred_element_type=F32
        )

    def chunk_rows(k):
        return pl.ds(pl.multiple_of(k * CHUNK, CHUNK), CHUNK)

    def peer_copy(k):
        rows = chunk_rows(k)
        return pltpu.make_async_remote_copy(
            src_ref=peer_tx.at[rows],
            dst_ref=peer_rx.at[rows],
            send_sem=peer_send.at[0],
            recv_sem=peer_recv.at[0],
            device_id={"dp": dp, "rep": other},
            device_id_type=MESH,
        )

    load_grads.wait()

    @pl.loop(0, CHUNKS)
    def _(k):
        peer_tx[chunk_rows(k)] = (product(k) * factor).astype(BF16)
        peer_copy(k).start()

    def for_own(lo, hi):
        @pl.loop(lo, hi)
        def _(k):
            rows = chunk_rows(k)
            own_g[rows] = product(k + CHUNKS) * factor + werr_v[rows].astype(F32)

    load_werr.wait()
    for_own(0, 4)

    def compress(lo, hi, place):
        @pl.loop(lo * 2, hi * 2)
        def _(t):
            dx, dy = place(t // 2)
            xx, yy = lax.rem(x + dx, NX), lax.rem(y + dy, NY)
            for k in range(NZ // 2):
                zz = lax.rem(t, 2) * (NZ // 2) + k
                rows = pl.ds(pl.multiple_of(dp_at(zz, yy, xx) * OWN, OWN), OWN)
                at = [(xx * RING + yy) * NZ + zz, (yy * RING + xx) * NZ + zz]
                combined = [
                    mom[i, at[i]].astype(F32) + own_g[rows, part.columns]
                    for i, part in enumerate(parts)
                ]
                size = jnp.abs(combined[0]) + jnp.abs(combined[1])
                scale = jnp.sum(size, axis=1, keepdims=True) * (1.0 / WIDTH) + tiny_scale
                inverse = 1.0 / scale
                for i, part in enumerate(parts):
                    codes = jnp.clip(combined[i] * inverse, -1.0, 1.0).astype(BF16)
                    decoded = codes.astype(F32) * scale
                    left_v[rows, part.columns] = (combined[i] - decoded).astype(BF16)
                    dec[i, at[i]] = decoded.astype(BF16)

    def skip_two(k):
        return k + k // 2

    def finish_gradient():
        for_own(4, 8)
        pltpu.make_async_copy(peer_rx, peer_rx, peer_recv.at[0]).wait()

    def compress_own():
        @pl.loop(0, HALF // 64)
        def _(t):
            rows = pl.ds(pl.multiple_of(t * 64, 64), 64)
            own_g[rows] += peer_rx[rows].astype(F32)

        compress(0, 1, lambda t: (0, 0))

    reduces = [
        Reduce(
            part, dec.at[i], z, 3 * i + 1, 4 * G_COUNT + i * R_COUNT, far.at[i],
            partial.at[i], mids.at[i], sums.at[i], rounded.at[i], firsts.at[i],
        )
        for i, part in enumerate(parts)
    ]

    def compress_near():
        compress(1, 9, lambda t: (skip_two(t // 3), skip_two(lax.rem(t, 3))))
        for row in (3, 1, 0):
            for r in reduces:
                r.last(row, 1)
                r.last(row, 3)

    def compress_far():
        compress(0, 4, lambda t: (2, t))
        compress(0, 3, lambda t: (skip_two(t), 2))

    gather_rest(gathers, finish_gradient, compress_own, compress_near, compress_far)
    for row in (2, 3, 1, 0):
        for r in reduces:
            r.last(row, 2)
            if row == 2:
                r.last(row, 1)
                r.last(row, 3)
    store_left = pltpu.make_async_copy(left_v, left_out, out_sems.at[0])
    store_left.start()

    @pl.loop(0, RING - 1)
    def _(t):
        row = lax.rem(2 + t, RING) + t // 2
        for r in reduces:
            r.mid(row)

    for r in reduces:
        r.mid_own()
    for r in reduces:
        r.first(dp_z)
    load_serr.wait()
    load_master.wait()
    load_variance.wait()
    summed = [r.total() for r in reduces]

    shifted = [
        summed[i] * (1.0 / (NX * NY * NZ)) + serr_v[:, part.columns]
        for i, part in enumerate(parts)
    ]
    size = jnp.abs(shifted[0]) + jnp.abs(shifted[1])
    scale = jnp.sum(size, axis=1, keepdims=True) * (1.0 / WIDTH) + tiny_scale
    gathers_w = []
    for i, part in enumerate(parts):
        codes = jnp.clip(shifted[i] / scale, -1.0, 1.0).astype(BF16)
        codes_v[:, part.columns] = codes
        momentum = codes.astype(F32) * scale
        server_v[:, part.columns] = shifted[i] - momentum
        new = master_v[:, part.columns] - learn_rate * momentum / (
            jnp.sqrt(variance_v[:, part.columns]) + tiny_root
        )
        new_master_v[:, part.columns] = new
        part.shard(wts.at[i], part.p, part.q, z)[...] = new.astype(BF16)
        g = Gather(part, wts.at[i], z, 3 * i + 2, (2 + i) * G_COUNT)
        g.first(dp_z)
        gathers_w.append(g)
    scale_out[...] = jnp.sum(
        jnp.where(eye, jnp.broadcast_to(scale, (OWN, OWN)), 0.0), axis=0, keepdims=True
    )
    stores = [
        store_left,
        pltpu.make_async_copy(codes_v, codes_out, out_sems.at[1]),
        pltpu.make_async_copy(server_v, server_out, out_sems.at[2]),
        pltpu.make_async_copy(new_master_v, master_out, out_sems.at[3]),
    ]
    for copy in stores[1:]:
        copy.start()

    def place(row):
        for i, g in enumerate(gathers_w):
            q = g.part.at_q(row)
            for p in range(RING):
                xx, yy = (p, q) if i == 0 else (q, p)
                pltpu.make_async_copy(
                    g.part.block(g.buf, p, q),
                    weights_out.at[:, yy, xx, :, pl.ds(i * PART, PART)],
                    out_sems.at[4],
                ).start()

    def place_near():
        for row in (0, 3, 1):
            place(row)

    gather_rest(gathers_w, lambda: None, lambda: None, place_near, lambda: place(2))
    pltpu.make_async_copy(weights_out, weights_out, out_sems.at[4]).wait()
    for copy in stores:
        copy.wait()
    for g in gathers + gathers_w + reduces:
        g.drain()
    pltpu.make_async_copy(peer_tx, peer_tx, peer_send.at[0]).wait()


def copy_kernel(count, *refs):
    sources, targets, sems = refs[:count], refs[count : 2 * count], refs[-1]
    copies = [pltpu.make_async_copy(sources[i], targets[i], sems.at[i]) for i in range(count)]
    for copy in copies:
        copy.start()
    for copy in copies:
        copy.wait()


def copied(arrays):
    return pl.pallas_call(
        functools.partial(copy_kernel, len(arrays)),
        out_shape=[jax.ShapeDtypeStruct(a.shape, a.dtype) for a in arrays],
        in_specs=[pl.BlockSpec(memory_space=pltpu.VMEM)] * len(arrays),
        out_specs=[pl.BlockSpec(memory_space=pltpu.HBM)] * len(arrays),
        scratch_shapes=[pltpu.SemaphoreType.DMA((len(arrays),))],
        compiler_params=pltpu.CompilerParams(vmem_limit_bytes=16 * 1024 * 1024),
        name="hand_out",
    )(*arrays)


def body(act, grads, werr, mcodes, mscale, serr, master, variance):
    tokens = act.shape[0]
    hbm = pl.BlockSpec(memory_space=pltpu.HBM)
    vmem = pl.BlockSpec(memory_space=pltpu.VMEM)
    shards = NX * NY * NZ
    tile = (OWN, PART)

    def vm(*shape, dtype=BF16):
        return pltpu.VMEM(shape, dtype)

    scratch = [
        vm(2 * CHUNKS, tokens, CHUNK),
        vm(tokens, WIDTH),
        vm(HALF, WIDTH),
        vm(OWN, WIDTH),
        vm(OWN, WIDTH, dtype=F32),
        vm(OWN, WIDTH, dtype=F32),
        vm(OWN, WIDTH, dtype=F32),
        vm(HALF, WIDTH),
        vm(OWN, WIDTH),
        vm(OWN, WIDTH, dtype=F32),
        vm(OWN, WIDTH, dtype=F32),
        vm(HALF, WIDTH, dtype=F32),
        vm(HALF, WIDTH),
        vm(HALF, WIDTH),
        vm(2, shards, *tile),
        vm(2, shards, *tile),
        vm(2, shards, *tile),
        vm(2, RING, (RING - 1) * NZ, *tile),
        vm(2, RING, NZ, *tile),
        vm(2, (RING - 1) * NZ, *tile),
        vm(2, NZ, *tile, dtype=F32),
        vm(2, NZ, *tile),
        vm(2, NZ - 1, *tile),
    ]
    dma = pltpu.SemaphoreType.DMA
    scratch += [
        dma((6,)),
        dma((2 * CHUNKS,)),
        dma((5,)),
        dma((1,)),
        dma((1,)),
        dma((6,)),
        dma((4 * G_COUNT + 2 * R_COUNT,)),
    ]
    shape = pltpu.VMEM
    outs = pl.pallas_call(
        step_kernel,
        out_shape=[
            shape((HALF, WIDTH), BF16),
            shape((OWN, WIDTH), BF16),
            shape((1, OWN), F32),
            shape((OWN, WIDTH), F32),
            shape((OWN, WIDTH), F32),
            shape((NZ, NY, NX, OWN, WIDTH), BF16),
        ],
        in_specs=[hbm] * 4 + [vmem] + [hbm] * 3,
        out_specs=[vmem] * 6,
        scratch_shapes=scratch,
        compiler_params=pltpu.CompilerParams(
            collective_id=0, has_side_effects=True, vmem_limit_bytes=54 * 1024 * 1024
        ),
        cost_estimate=pl.CostEstimate(
            flops=2 * tokens * 2 * HALF * WIDTH, bytes_accessed=14_000_000, transcendentals=0
        ),
        name="adam_step",
    )(act, grads, werr[0], mcodes, mscale.reshape(1, OWN), serr, master, variance)
    outs = [*outs[:-1], outs[-1].reshape(HALF, WIDTH)]
    left, codes, scale, server, new_master, weights = copied(outs)
    return (
        left[None],
        codes,
        scale.reshape(OWN),
        server,
        new_master,
        weights,
    )


def solution(mesh):
    return jax.shard_map(
        body,
        mesh=mesh,
        in_specs=(
            P(("dp", "rep"), None),
            P(("dp", "rep"), None),
            P("dp", "rep", None),
            P(("rep", "dp"), None),
            P(("rep", "dp")),
            P(("rep", "dp"), None),
            P(("rep", "dp"), None),
            P(("rep", "dp"), None),
        ),
        out_specs=(
            P("dp", "rep", None),
            P(("rep", "dp"), None),
            P(("rep", "dp")),
            P(("rep", "dp"), None),
            P(("rep", "dp"), None),
            P("rep", None),
        ),
        check_vma=False,
    )
```

```python
import functools
import math

import jax
import jax.numpy as jnp
from jax import lax
from jax.experimental import pallas as pl
from jax.experimental.pallas import tpu as pltpu
from jax.sharding import PartitionSpec as P

BF16 = jnp.bfloat16
F32 = jnp.float32
MESH = pl.DeviceIdType.MESH

NX, NY, NZ = 4, 4, 8
RING = 4
OWN = 16
GROUPS = 2
ROWS = OWN // GROUPS
PART = 256
LANES = PART // GROUPS
CHUNK = 256
HALF = 2048
WIDTH = 512
CHUNKS = HALF // CHUNK

beta_one = 0.9
learn_rate = 0.02
grad_boost = 8.0
tiny_scale = 1e-06
tiny_root = 1e-08


class Part:
    def __init__(self, group, column, p, q, dp_pq, core, send_sems, recv_sems):
        self.rows = slice(group * ROWS, (group + 1) * ROWS)
        self.columns = slice(column, column + PART)
        self.p, self.q, self.dp_pq, self.core = p, q, dp_pq, core
        self.send_sems, self.recv_sems = send_sems, recv_sems

    def at_p(self, k):
        return lax.rem(self.p + (k + RING), RING)

    def at_q(self, k):
        return lax.rem(self.q + (k + RING), RING)

    def shard(self, buf, p, q, z):
        return buf.at[(p * RING + q) * NZ + z]

    def block(self, buf, p, q):
        return buf.at[pl.ds((p * RING + q) * NZ, NZ)]

    def half(self, buf, p, q, which):
        return buf.at[pl.ds((p * RING + q) * NZ + which * (NZ // 2), NZ // 2)]

    def send(self, src, dst, send, recv, dp):
        pltpu.make_async_remote_copy(
            src_ref=src,
            dst_ref=dst,
            send_sem=self.send_sems.at[send],
            recv_sem=self.recv_sems.at[recv],
            device_id={"dp": dp, "rep": self.core},
            device_id_type=MESH,
        ).start()

    def wait(self, like, recv):
        pltpu.make_async_copy(like, like, self.recv_sems.at[recv]).wait()

    def drain(self, like, send):
        pltpu.make_async_copy(like, like, self.send_sems.at[send]).wait()


G_FIRST, G_MID, G_ROW, G_COUNT = 0, 0, 4, 8
R_FIRST, R_MID, R_ROW, R_COUNT = 0, 1, 2, 6


def packed(rows):
    return jnp.concatenate([rows[:, :LANES], rows[:, LANES:]], axis=0).astype(BF16)


def unpacked_sum(wide):
    return jnp.concatenate([wide[:ROWS], wide[ROWS:]], axis=1)


def unpacked(tile):
    return unpacked_sum(tile.astype(F32))


class Gather:
    def __init__(self, part, buf, z, send, recv):
        self.part, self.buf, self.z, self.send_sem, self.recv = part, buf, z, send, recv

    def go(self, src, dst_recv, dp):
        self.part.send(src, src, self.send_sem, self.recv + dst_recv, dp)

    def first(self, dp_z):
        mine = self.part.shard(self.buf, self.part.p, self.part.q, self.z)
        for k in (4, 3, 5, 2, 6, 1, 7):
            self.go(mine, G_FIRST, dp_z(lax.rem(self.z + k, NZ)))

    def first_here(self):
        self.part.wait(self.buf.at[pl.ds(0, NZ - 1)], self.recv + G_FIRST)

    def mid(self):
        part = self.part
        for k in (2, 1, 3):
            self.go(part.block(self.buf, part.p, part.q), G_MID + k, part.dp_pq(part.p, part.at_q(k)))

    def mid_here(self, k):
        part = self.part
        part.wait(part.block(self.buf, part.p, part.at_q(-k)), self.recv + G_MID + k)

    def last(self, row):
        part = self.part
        block = part.block(self.buf, part.p, part.at_q(row))
        for k in (2, 1, 3):
            self.go(block, G_ROW + row, part.dp_pq(part.at_p(k), part.q))

    def row_here(self, row):
        self.part.wait(self.buf.at[pl.ds(0, 3 * NZ)], self.recv + G_ROW + row)

    def drain(self):
        self.part.drain(self.buf.at[pl.ds(0, NX * NY * NZ - 1)], self.send_sem)


def begin(gathers):
    for g in gathers:
        g.first_here()
    for g in gathers:
        g.mid()
        g.last(0)


def spread(gathers):
    for k in (1, 3, 2):
        for g in gathers:
            g.mid_here(k)
            g.last(RING - k)


def here(gathers, rows):
    for row in rows:
        for g in gathers:
            g.row_here(row)


class Reduce:
    def __init__(self, part, dec, z, send, recv, far, partial, mids, sums, rounded, firsts):
        self.part, self.dec, self.z, self.send_sem, self.recv = part, dec, z, send, recv
        self.far, self.partial = far, partial
        self.mids, self.sums, self.rounded, self.firsts = mids, sums, rounded, firsts

    def go(self, src, dst, recv, dp):
        self.part.send(src, dst, self.send_sem, self.recv + recv, dp)

    def last(self, row, k):
        part = self.part
        self.go(
            part.block(self.dec, part.at_p(k), part.at_q(row)),
            self.far.at[row, pl.ds((k - 1) * NZ, NZ)],
            R_ROW + row,
            part.dp_pq(part.at_p(k), part.q),
        )

    def row_total(self, row):
        part = self.part
        part.wait(self.far.at[row], self.recv + R_ROW + row)
        total = part.block(self.dec, part.p, part.at_q(row))[...].astype(F32)
        for k in range(RING - 1):
            total += self.far[row, pl.ds(k * NZ, NZ)].astype(F32)
        return total

    def mid(self, row):
        part = self.part
        self.partial[row] = self.row_total(row).astype(BF16)
        self.go(
            self.partial.at[row],
            self.mids.at[pl.ds((row - 1) * NZ, NZ)],
            R_MID,
            part.dp_pq(part.p, part.at_q(row)),
        )

    def mid_own(self):
        self.sums[...] = self.row_total(0)

    def first(self, dp_z):
        self.part.wait(self.mids, self.recv + R_MID)
        total = self.sums[...]
        for k in range(RING - 1):
            total += self.mids[pl.ds(k * NZ, NZ)].astype(F32)
        self.sums[...] = total
        self.rounded[...] = total.astype(BF16)
        for k in range(1, NZ):
            to = lax.rem(self.z + k, NZ)
            self.go(self.rounded.at[to], self.firsts.at[k - 1], R_FIRST, dp_z(to))

    def total(self):
        self.part.wait(self.firsts, self.recv + R_FIRST)
        total = self.sums[self.z]
        for k in range(NZ - 1):
            total += self.firsts[k].astype(F32)
        return total

    def drain(self):
        self.part.drain(self.dec.at[pl.ds(0, NX * NY * NZ - 1)], self.send_sem)


def step_kernel(
    act, grads, werr, mcodes, mscale, serr, master, variance,
    left_out, codes_out, scale_out, server_out, master_out, weights_out,
    act_v, grads_v, werr_v, mcodes_v, serr_v, master_v, variance_v,
    own_g, left_v, peer_tx, peer_rx,
    mom, dec, wts, far, partial, mids, sums, rounded, firsts,
    in_sems, act_sems, peer_send, peer_recv, send_sems, recv_sems,
):
    dp = lax.axis_index("dp")
    core = lax.axis_index("rep")
    x = lax.rem(dp, NX)
    y = lax.rem(dp // NX, NY)
    z = dp // (NX * NY)
    other = 1 - core
    tokens = act.shape[0]
    factor = (1.0 - beta_one) * grad_boost / math.sqrt(2 * tokens)

    def load(k, src, dst):
        copy = pltpu.make_async_copy(src, dst, in_sems.at[k])
        copy.start()
        return copy

    load_codes = load(0, mcodes, mcodes_v)

    def dp_at(zz, yy, xx):
        return zz * (NX * NY) + yy * NX + xx

    def dp_z(zz):
        return dp_at(zz, y, x)

    barrier = pltpu.get_barrier_semaphore()
    peers = [(dp_at(lax.rem(z + k, NZ), y, x), core) for k in range(1, NZ)]
    peers += [(dp_at(z, y, lax.rem(x + k, NX)), core) for k in range(1, NX)]
    peers += [(dp_at(z, lax.rem(y + k, NY), x), core) for k in range(1, NY)]
    peers += [(dp, other)]
    for peer_dp, peer_core in peers:
        pl.semaphore_signal(
            barrier, inc=1, device_id={"dp": peer_dp, "rep": peer_core}, device_id_type=MESH
        )

    load_grads = load(1, grads, grads_v)

    def act_copy(k):
        base = jnp.where(k < CHUNKS, other * HALF, core * HALF)
        column = pl.multiple_of(base + lax.rem(k, CHUNKS) * CHUNK, CHUNK)
        return pltpu.make_async_copy(
            act.at[:, pl.ds(column, CHUNK)], act_v.at[k], act_sems.at[k]
        )

    @pl.loop(0, 2 * CHUNKS)
    def _(k):
        act_copy(k).start()

    load_werr = load(2, werr, werr_v)
    load_serr = load(3, serr, serr_v)
    load_master = load(4, master, master_v)
    load_variance = load(5, variance, variance_v)

    eye = lax.broadcasted_iota(jnp.int32, (OWN, OWN), 0) == lax.broadcasted_iota(
        jnp.int32, (OWN, OWN), 1
    )
    scale_col = jnp.sum(
        jnp.where(eye, jnp.broadcast_to(mscale[...], (OWN, OWN)), 0.0), axis=1, keepdims=True
    )
    load_codes.wait()
    previous = mcodes_v[...].astype(F32) * (beta_one * scale_col)

    def x_major(p, q):
        return dp_at(z, q, p)

    def y_major(p, q):
        return dp_at(z, p, q)

    parts = []
    for group in range(GROUPS):
        parts += [
            Part(group, 0, x, y, x_major, core, send_sems, recv_sems),
            Part(group, PART, y, x, y_major, core, send_sems, recv_sems),
        ]
    count = len(parts)

    def by_group(items):
        return [items[2 * group : 2 * group + 2] for group in range(GROUPS)]

    gathers, gathers_w, reduces = [], [], []
    for n, part in enumerate(parts):
        part.shard(mom.at[n], part.p, part.q, z)[...] = packed(previous[part.rows, part.columns])
        gathers.append(Gather(part, mom.at[n], z, 3 * n, n * G_COUNT))
        gathers_w.append(Gather(part, wts.at[n], z, 3 * n + 2, (count + n) * G_COUNT))
        reduces.append(
            Reduce(
                part, dec.at[n], z, 3 * n + 1, 2 * count * G_COUNT + n * R_COUNT, far.at[n],
                partial.at[n], mids.at[n], sums.at[n], rounded.at[n], firsts.at[n],
            )
        )
    pl.semaphore_wait(barrier, len(peers))
    for g in gathers:
        g.first(dp_z)

    def product(k):
        act_copy(k).wait()
        return lax.dot_general(
            act_v[k], grads_v[...], (((0,), (0,)), ((), ())), preferred_element_type=F32
        )

    def chunk_rows(k):
        return pl.ds(pl.multiple_of(k * CHUNK, CHUNK), CHUNK)

    def peer_copy(k):
        rows = chunk_rows(k)
        return pltpu.make_async_remote_copy(
            src_ref=peer_tx.at[rows],
            dst_ref=peer_rx.at[rows],
            send_sem=peer_send.at[0],
            recv_sem=peer_recv.at[0],
            device_id={"dp": dp, "rep": other},
            device_id_type=MESH,
        )

    load_grads.wait()

    @pl.loop(0, CHUNKS)
    def _(k):
        peer_tx[chunk_rows(k)] = (product(k) * factor).astype(BF16)
        peer_copy(k).start()

    def for_own(lo, hi):
        @pl.loop(lo, hi)
        def _(k):
            rows = chunk_rows(k)
            own_g[rows] = product(k + CHUNKS) * factor + werr_v[rows].astype(F32)

    load_werr.wait()
    for_own(0, 4)

    for gs in by_group(gathers):
        begin(gs)
    for_own(4, 8)
    for gs in by_group(gathers):
        spread(gs)
    pltpu.make_async_copy(peer_rx, peer_rx, peer_recv.at[0]).wait()

    @pl.loop(0, HALF // 64)
    def _(t):
        rows = pl.ds(pl.multiple_of(t * 64, 64), 64)
        own_g[rows] += peer_rx[rows].astype(F32)

    def blocks(lo, hi, offsets, work):
        @pl.loop(lo, hi)
        def _(t):
            dx, dy = offsets(t)
            xx, yy = lax.rem(x + dx, NX), lax.rem(y + dy, NY)
            work(yy, xx, [(xx * RING + yy) * NZ, (yy * RING + xx) * NZ])

    def skip_two(k):
        return k + k // 2

    def near_blocks(work):
        blocks(0, 9, lambda t: (skip_two(t // 3), skip_two(lax.rem(t, 3))), work)

    def far_blocks(work):
        blocks(0, 4, lambda t: (2, t), work)
        blocks(0, 3, lambda t: (skip_two(t), 2), work)

    def compress(group, yy, xx, at):
        rows = [
            pl.ds(pl.multiple_of(dp_at(zz, yy, xx) * OWN + group * ROWS, ROWS), ROWS)
            for zz in range(NZ)
        ]
        pair = (0, 1)
        combined = [
            [
                unpacked(mom[2 * group + i, at[i] + zz]) + own_g[rows[zz], parts[i].columns]
                for i in pair
            ]
            for zz in range(NZ)
        ]
        scales = []
        for zz in range(NZ):
            size = jnp.abs(combined[zz][0]) + jnp.abs(combined[zz][1])
            total = jnp.sum(size, axis=1, keepdims=True)
            scales.append(total * (1.0 / WIDTH) + tiny_scale)
        for zz in range(NZ):
            inverse = 1.0 / scales[zz]
            for i in pair:
                codes = jnp.clip(combined[zz][i] * inverse, -1.0, 1.0).astype(BF16)
                decoded = codes.astype(F32) * scales[zz]
                left_v[rows[zz], parts[i].columns] = combined[zz][i] - decoded
                dec[2 * group + i, at[i] + zz] = packed(decoded)

    near_rows = (0, 3, 1)
    for group, (gs, rs) in enumerate(zip(by_group(gathers), by_group(reduces))):
        work = functools.partial(compress, group)
        here(gs, near_rows)
        near_blocks(work)
        for row in (3, 1, 0):
            for r in rs:
                r.last(row, 1)
                r.last(row, 3)
        here(gs, (2,))
        far_blocks(work)
        for row in (2, 3, 1, 0):
            for r in rs:
                r.last(row, 2)
                if row == 2:
                    r.last(row, 1)
                    r.last(row, 3)

    @pl.loop(0, HALF // 64)
    def _(t):
        rows = pl.ds(pl.multiple_of(t * 64, 64), 64)
        left_out[rows] = left_v[rows].astype(BF16)

    for rs in by_group(reduces):

        @pl.loop(0, RING - 1)
        def _(t):
            row = lax.rem(2 + t, RING) + t // 2
            for r in rs:
                r.mid(row)

        for r in rs:
            r.mid_own()
    for rs in by_group(reduces):
        for r in rs:
            r.first(dp_z)
    load_serr.wait()
    load_master.wait()
    load_variance.wait()

    all_codes, all_scales = [], []
    for group, (gs, rs) in enumerate(zip(by_group(gathers_w), by_group(reduces))):
        rows = parts[2 * group].rows
        shifted = [
            unpacked_sum(r.total()) * (1.0 / (NX * NY * NZ)) + serr_v[rows, r.part.columns]
            for r in rs
        ]
        size = jnp.abs(shifted[0]) + jnp.abs(shifted[1])
        scale = jnp.sum(size, axis=1, keepdims=True) * (1.0 / WIDTH) + tiny_scale
        for i, g in enumerate(gs):
            columns = g.part.columns
            codes = jnp.clip(shifted[i] / scale, -1.0, 1.0).astype(BF16).astype(F32)
            all_codes.append(codes)
            momentum = codes * scale
            server_out[rows, columns] = shifted[i] - momentum
            new = master_v[rows, columns] - learn_rate * momentum / (
                jnp.sqrt(variance_v[rows, columns]) + tiny_root
            )
            master_out[rows, columns] = new
            g.part.shard(g.buf, g.part.p, g.part.q, z)[...] = packed(new)
            g.first(dp_z)
        all_scales.append(scale)
    for i in range(2):
        codes_out[:, parts[i].columns] = jnp.concatenate(all_codes[i::2], axis=0).astype(BF16)
    scale = jnp.concatenate(all_scales, axis=0)
    scale_out[...] = jnp.sum(
        jnp.where(eye, jnp.broadcast_to(scale, (OWN, OWN)), 0.0), axis=0, keepdims=True
    )

    def assemble(yy, xx, at):
        for zz in range(NZ):
            for i in range(2):
                rows = [unpacked(wts[2 * group + i, at[i] + zz]) for group in range(GROUPS)]
                weights_out[zz, yy, xx, :, parts[i].columns] = jnp.concatenate(
                    rows, axis=0
                ).astype(BF16)

    for gs in by_group(gathers_w):
        begin(gs)
    for gs in by_group(gathers_w):
        spread(gs)
    here(gathers_w, near_rows)
    near_blocks(assemble)
    here(gathers_w, (2,))
    far_blocks(assemble)
    for g in gathers + gathers_w + reduces:
        g.drain()
    pltpu.make_async_copy(peer_tx, peer_tx, peer_send.at[0]).wait()


def copy_kernel(count, *refs):
    sources, targets, sems = refs[:count], refs[count : 2 * count], refs[-1]
    copies = [pltpu.make_async_copy(sources[i], targets[i], sems.at[i]) for i in range(count)]
    for copy in copies:
        copy.start()
    for copy in copies:
        copy.wait()


def copied(arrays):
    return pl.pallas_call(
        functools.partial(copy_kernel, len(arrays)),
        out_shape=[jax.ShapeDtypeStruct(a.shape, a.dtype) for a in arrays],
        in_specs=[pl.BlockSpec(memory_space=pltpu.VMEM)] * len(arrays),
        out_specs=[pl.BlockSpec(memory_space=pltpu.HBM)] * len(arrays),
        scratch_shapes=[pltpu.SemaphoreType.DMA((len(arrays),))],
        compiler_params=pltpu.CompilerParams(vmem_limit_bytes=16 * 1024 * 1024),
        name="hand_out",
    )(*arrays)


def body(act, grads, werr, mcodes, mscale, serr, master, variance):
    tokens = act.shape[0]
    hbm = pl.BlockSpec(memory_space=pltpu.HBM)
    vmem = pl.BlockSpec(memory_space=pltpu.VMEM)
    shards = NX * NY * NZ
    tile = (OWN, LANES)
    count = 2 * GROUPS

    def vm(*shape, dtype=BF16):
        return pltpu.VMEM(shape, dtype)

    scratch = [
        vm(2 * CHUNKS, tokens, CHUNK),
        vm(tokens, WIDTH),
        vm(HALF, WIDTH),
        vm(OWN, WIDTH),
        vm(OWN, WIDTH, dtype=F32),
        vm(OWN, WIDTH, dtype=F32),
        vm(OWN, WIDTH, dtype=F32),
        vm(HALF, WIDTH, dtype=F32),
        vm(HALF, WIDTH, dtype=F32),
        vm(HALF, WIDTH),
        vm(HALF, WIDTH),
        vm(count, shards, *tile),
        vm(count, shards, *tile),
        vm(count, shards, *tile),
        vm(count, RING, (RING - 1) * NZ, *tile),
        vm(count, RING, NZ, *tile),
        vm(count, (RING - 1) * NZ, *tile),
        vm(count, NZ, *tile, dtype=F32),
        vm(count, NZ, *tile),
        vm(count, NZ - 1, *tile),
    ]
    dma = pltpu.SemaphoreType.DMA
    scratch += [
        dma((6,)),
        dma((2 * CHUNKS,)),
        dma((1,)),
        dma((1,)),
        dma((3 * count,)),
        dma((2 * count * G_COUNT + count * R_COUNT,)),
    ]
    shape = pltpu.VMEM
    outs = pl.pallas_call(
        step_kernel,
        out_shape=[
            shape((HALF, WIDTH), BF16),
            shape((OWN, WIDTH), BF16),
            shape((1, OWN), F32),
            shape((OWN, WIDTH), F32),
            shape((OWN, WIDTH), F32),
            shape((NZ, NY, NX, OWN, WIDTH), BF16),
        ],
        in_specs=[hbm] * 4 + [vmem] + [hbm] * 3,
        out_specs=[vmem] * 6,
        scratch_shapes=scratch,
        compiler_params=pltpu.CompilerParams(
            collective_id=0, has_side_effects=True, vmem_limit_bytes=54 * 1024 * 1024
        ),
        cost_estimate=pl.CostEstimate(
            flops=2 * tokens * 2 * HALF * WIDTH, bytes_accessed=14_000_000, transcendentals=0
        ),
        name="adam_step",
    )(act, grads, werr[0], mcodes, mscale.reshape(1, OWN), serr, master, variance)
    outs = [*outs[:-1], outs[-1].reshape(HALF, WIDTH)]
    left, codes, scale, server, new_master, weights = copied(outs)
    return (
        left[None],
        codes,
        scale.reshape(OWN),
        server,
        new_master,
        weights,
    )


def solution(mesh):
    return jax.shard_map(
        body,
        mesh=mesh,
        in_specs=(
            P(("dp", "rep"), None),
            P(("dp", "rep"), None),
            P("dp", "rep", None),
            P(("rep", "dp"), None),
            P(("rep", "dp")),
            P(("rep", "dp"), None),
            P(("rep", "dp"), None),
            P(("rep", "dp"), None),
        ),
        out_specs=(
            P("dp", "rep", None),
            P(("rep", "dp"), None),
            P(("rep", "dp")),
            P(("rep", "dp"), None),
            P(("rep", "dp"), None),
            P("rep", None),
        ),
        check_vma=False,
    )
```

```python
import functools
import math

import jax
import jax.numpy as jnp
from jax import lax
from jax.experimental import pallas as pl
from jax.experimental.pallas import tpu as pltpu
from jax.sharding import PartitionSpec as P

BF16 = jnp.bfloat16
F32 = jnp.float32
MESH = pl.DeviceIdType.MESH

NX, NY, NZ = 4, 4, 8
RING = 4
OWN = 16
GROUPS = 2
ROWS = OWN // GROUPS
PART = 256
LANES = PART // GROUPS
CHUNK = 256
HALF = 2048
WIDTH = 512
CHUNKS = HALF // CHUNK

beta_one = 0.9
learn_rate = 0.02
grad_boost = 8.0
tiny_scale = 1e-06
tiny_root = 1e-08


class Part:
    def __init__(self, group, column, p, q, dp_pq, core, send_sems, recv_sems):
        self.rows = slice(group * ROWS, (group + 1) * ROWS)
        self.columns = slice(column, column + PART)
        self.p, self.q, self.dp_pq, self.core = p, q, dp_pq, core
        self.send_sems, self.recv_sems = send_sems, recv_sems

    def at_p(self, k):
        return lax.rem(self.p + (k + RING), RING)

    def at_q(self, k):
        return lax.rem(self.q + (k + RING), RING)

    def shard(self, buf, p, q, z):
        return buf.at[(p * RING + q) * NZ + z]

    def block(self, buf, p, q):
        return buf.at[pl.ds((p * RING + q) * NZ, NZ)]

    def half(self, buf, p, q, which):
        return buf.at[pl.ds((p * RING + q) * NZ + which * (NZ // 2), NZ // 2)]

    def send(self, src, dst, send, recv, dp):
        pltpu.make_async_remote_copy(
            src_ref=src,
            dst_ref=dst,
            send_sem=self.send_sems.at[send],
            recv_sem=self.recv_sems.at[recv],
            device_id={"dp": dp, "rep": self.core},
            device_id_type=MESH,
        ).start()

    def wait(self, like, recv):
        pltpu.make_async_copy(like, like, self.recv_sems.at[recv]).wait()

    def drain(self, like, send):
        pltpu.make_async_copy(like, like, self.send_sems.at[send]).wait()


G_FIRST, G_MID, G_ROW, G_LEFT, G_RIGHT, G_COUNT = 0, 0, 4, 8, 9, 10
R_FIRST, R_MID, R_ROW, R_COUNT = 0, 1, 2, 6


def packed(rows):
    return jnp.concatenate([rows[:, :LANES], rows[:, LANES:]], axis=0).astype(BF16)


def unpacked_sum(wide):
    return jnp.concatenate([wide[:ROWS], wide[ROWS:]], axis=1)


def unpacked(tile):
    return unpacked_sum(tile.astype(F32))


NEAR = (0,)


class Gather:
    def __init__(self, part, buf, z, send, recv):
        self.part, self.buf, self.z, self.send_sem, self.recv = part, buf, z, send, recv

    def go(self, src, dst_recv, dp):
        self.part.send(src, src, self.send_sem, self.recv + dst_recv, dp)

    def first(self, dp_z):
        mine = self.part.shard(self.buf, self.part.p, self.part.q, self.z)
        for k in (4, 3, 5, 2, 6, 1, 7):
            self.go(mine, G_FIRST, dp_z(lax.rem(self.z + k, NZ)))

    def first_here(self):
        self.part.wait(self.buf.at[pl.ds(0, NZ - 1)], self.recv + G_FIRST)

    def mid(self):
        part = self.part
        for k in (2, 1, 3):
            self.go(part.block(self.buf, part.p, part.q), G_MID + k, part.dp_pq(part.p, part.at_q(k)))

    def mid_here(self, k):
        part = self.part
        part.wait(part.block(self.buf, part.p, part.at_q(-k)), self.recv + G_MID + k)

    def last(self, row):
        part = self.part
        block = part.block(self.buf, part.p, part.at_q(row))
        for k in (2, 1, 3):
            self.go(block, G_ROW + row, part.dp_pq(part.at_p(k), part.q))

    def halves(self, p, row):
        q = self.part.at_q(row)
        return self.part.half(self.buf, p, q, 0), self.part.half(self.buf, p, q, 1)

    def last_near(self, row):
        part = self.part
        lower, upper = self.halves(part.p, row)
        after, before = part.dp_pq(part.at_p(1), part.q), part.dp_pq(part.at_p(-1), part.q)
        slot = NEAR.index(row)
        self.go(lower, G_LEFT + slot, after)
        self.go(upper, G_RIGHT + slot, before)
        self.go(upper, G_ROW + row, after)
        self.go(lower, G_ROW + row, before)

    def relay(self, row):
        part = self.part
        slot = NEAR.index(row)
        lower = self.halves(part.at_p(-1), row)[0]
        part.wait(lower, self.recv + G_LEFT + slot)
        self.go(lower, G_ROW + row, part.dp_pq(part.at_p(1), part.q))
        upper = self.halves(part.at_p(1), row)[1]
        part.wait(upper, self.recv + G_RIGHT + slot)
        self.go(upper, G_ROW + row, part.dp_pq(part.at_p(-1), part.q))

    def row_here(self, row):
        blocks = 3 if row not in NEAR else 2
        self.part.wait(self.buf.at[pl.ds(0, blocks * NZ)], self.recv + G_ROW + row)

    def drain(self):
        self.part.drain(self.buf.at[pl.ds(0, NX * NY * NZ - 1)], self.send_sem)


def begin(gathers):
    for g in gathers:
        g.first_here()
        g.mid()
    for g in gathers:
        g.last_near(0)


def spread(gathers):
    for k in (1, 3):
        for g in gathers:
            g.mid_here(k)
            g.last(RING - k)
    for g in gathers:
        g.relay(0)
    for g in gathers:
        g.mid_here(2)
        g.last(2)


def here(gathers, rows):
    for row in rows:
        for g in gathers:
            g.row_here(row)


class Reduce:
    def __init__(self, part, dec, z, send, recv, far, partial, mids, sums, rounded, firsts):
        self.part, self.dec, self.z, self.send_sem, self.recv = part, dec, z, send, recv
        self.far, self.partial = far, partial
        self.mids, self.sums, self.rounded, self.firsts = mids, sums, rounded, firsts

    def go(self, src, dst, recv, dp):
        self.part.send(src, dst, self.send_sem, self.recv + recv, dp)

    def last(self, row, k):
        part = self.part
        self.go(
            part.block(self.dec, part.at_p(k), part.at_q(row)),
            self.far.at[row, pl.ds((k - 1) * NZ, NZ)],
            R_ROW + row,
            part.dp_pq(part.at_p(k), part.q),
        )

    def row_total(self, row):
        part = self.part
        part.wait(self.far.at[row], self.recv + R_ROW + row)
        total = part.block(self.dec, part.p, part.at_q(row))[...].astype(F32)
        for k in range(RING - 1):
            total += self.far[row, pl.ds(k * NZ, NZ)].astype(F32)
        return total

    def mid(self, row):
        part = self.part
        self.partial[row] = self.row_total(row).astype(BF16)
        self.go(
            self.partial.at[row],
            self.mids.at[pl.ds((row - 1) * NZ, NZ)],
            R_MID,
            part.dp_pq(part.p, part.at_q(row)),
        )

    def mid_own(self):
        self.sums[...] = self.row_total(0)

    def first(self, dp_z):
        self.part.wait(self.mids, self.recv + R_MID)
        total = self.sums[...]
        for k in range(RING - 1):
            total += self.mids[pl.ds(k * NZ, NZ)].astype(F32)
        self.sums[...] = total
        self.rounded[...] = total.astype(BF16)
        for k in range(1, NZ):
            to = lax.rem(self.z + k, NZ)
            self.go(self.rounded.at[to], self.firsts.at[k - 1], R_FIRST, dp_z(to))

    def total(self):
        self.part.wait(self.firsts, self.recv + R_FIRST)
        total = self.sums[self.z]
        for k in range(NZ - 1):
            total += self.firsts[k].astype(F32)
        return total

    def drain(self):
        self.part.drain(self.dec.at[pl.ds(0, NX * NY * NZ - 1)], self.send_sem)


def step_kernel(
    act, grads, werr, mcodes, mscale, serr, master, variance,
    left_out, codes_out, scale_out, server_out, master_out, weights_out,
    act_v, grads_v, werr_v, mcodes_v, serr_v, master_v, variance_v,
    own_g, left_v, peer_tx, peer_rx,
    mom, dec, wts, far, partial, mids, sums, rounded, firsts,
    in_sems, act_sems, peer_send, peer_recv, send_sems, recv_sems,
):
    dp = lax.axis_index("dp")
    core = lax.axis_index("rep")
    x = lax.rem(dp, NX)
    y = lax.rem(dp // NX, NY)
    z = dp // (NX * NY)
    other = 1 - core
    tokens = act.shape[0]
    factor = (1.0 - beta_one) * grad_boost / math.sqrt(2 * tokens)

    def load(k, src, dst):
        copy = pltpu.make_async_copy(src, dst, in_sems.at[k])
        copy.start()
        return copy

    load_codes = load(0, mcodes, mcodes_v)

    def dp_at(zz, yy, xx):
        return zz * (NX * NY) + yy * NX + xx

    def dp_z(zz):
        return dp_at(zz, y, x)

    barrier = pltpu.get_barrier_semaphore()
    peers = [(dp_at(lax.rem(z + k, NZ), y, x), core) for k in range(1, NZ)]
    peers += [(dp_at(z, y, lax.rem(x + k, NX)), core) for k in range(1, NX)]
    peers += [(dp_at(z, lax.rem(y + k, NY), x), core) for k in range(1, NY)]
    peers += [(dp, other)]
    for peer_dp, peer_core in peers:
        pl.semaphore_signal(
            barrier, inc=1, device_id={"dp": peer_dp, "rep": peer_core}, device_id_type=MESH
        )

    load_grads = load(1, grads, grads_v)

    def act_copy(k):
        base = jnp.where(k < CHUNKS, other * HALF, core * HALF)
        column = pl.multiple_of(base + lax.rem(k, CHUNKS) * CHUNK, CHUNK)
        return pltpu.make_async_copy(
            act.at[:, pl.ds(column, CHUNK)], act_v.at[k], act_sems.at[k]
        )

    @pl.loop(0, 2 * CHUNKS)
    def _(k):
        act_copy(k).start()

    load_werr = load(2, werr, werr_v)
    load_serr = load(3, serr, serr_v)
    load_master = load(4, master, master_v)
    load_variance = load(5, variance, variance_v)

    eye = lax.broadcasted_iota(jnp.int32, (OWN, OWN), 0) == lax.broadcasted_iota(
        jnp.int32, (OWN, OWN), 1
    )
    scale_col = jnp.sum(
        jnp.where(eye, jnp.broadcast_to(mscale[...], (OWN, OWN)), 0.0), axis=1, keepdims=True
    )
    load_codes.wait()
    previous = mcodes_v[...].astype(F32) * (beta_one * scale_col)

    def x_major(p, q):
        return dp_at(z, q, p)

    def y_major(p, q):
        return dp_at(z, p, q)

    parts = []
    for group in range(GROUPS):
        parts += [
            Part(group, 0, x, y, x_major, core, send_sems, recv_sems),
            Part(group, PART, y, x, y_major, core, send_sems, recv_sems),
        ]
    count = len(parts)

    def by_group(items):
        return [items[2 * group : 2 * group + 2] for group in range(GROUPS)]

    gathers, gathers_w, reduces = [], [], []
    for n, part in enumerate(parts):
        part.shard(mom.at[n], part.p, part.q, z)[...] = packed(previous[part.rows, part.columns])
        gathers.append(Gather(part, mom.at[n], z, 3 * n, n * G_COUNT))
        gathers_w.append(Gather(part, wts.at[n], z, 3 * n + 2, (count + n) * G_COUNT))
        reduces.append(
            Reduce(
                part, dec.at[n], z, 3 * n + 1, 2 * count * G_COUNT + n * R_COUNT, far.at[n],
                partial.at[n], mids.at[n], sums.at[n], rounded.at[n], firsts.at[n],
            )
        )
    pl.semaphore_wait(barrier, len(peers))
    for g in gathers:
        g.first(dp_z)

    def product(k):
        act_copy(k).wait()
        return lax.dot_general(
            act_v[k], grads_v[...], (((0,), (0,)), ((), ())), preferred_element_type=F32
        )

    def chunk_rows(k):
        return pl.ds(pl.multiple_of(k * CHUNK, CHUNK), CHUNK)

    def peer_copy(k):
        rows = chunk_rows(k)
        return pltpu.make_async_remote_copy(
            src_ref=peer_tx.at[rows],
            dst_ref=peer_rx.at[rows],
            send_sem=peer_send.at[0],
            recv_sem=peer_recv.at[0],
            device_id={"dp": dp, "rep": other},
            device_id_type=MESH,
        )

    load_grads.wait()

    @pl.loop(0, CHUNKS)
    def _(k):
        peer_tx[chunk_rows(k)] = (product(k) * factor).astype(BF16)
        peer_copy(k).start()

    def for_own(lo, hi):
        @pl.loop(lo, hi)
        def _(k):
            rows = chunk_rows(k)
            own_g[rows] = product(k + CHUNKS) * factor + werr_v[rows].astype(F32)

    begin(gathers)
    load_werr.wait()
    for_own(0, 6)
    for gs in by_group(gathers):
        spread(gs)
    for_own(6, 8)
    pltpu.make_async_copy(peer_rx, peer_rx, peer_recv.at[0]).wait()

    @pl.loop(0, HALF // 64)
    def _(t):
        rows = pl.ds(pl.multiple_of(t * 64, 64), 64)
        own_g[rows] += peer_rx[rows].astype(F32)

    def blocks(lo, hi, offsets, work):
        @pl.loop(lo, hi)
        def _(t):
            dx, dy = offsets(t)
            xx, yy = lax.rem(x + dx, NX), lax.rem(y + dy, NY)
            work(yy, xx, [(xx * RING + yy) * NZ, (yy * RING + xx) * NZ])

    def skip_two(k):
        return k + k // 2

    def near_blocks(work):
        blocks(0, 9, lambda t: (skip_two(t // 3), skip_two(lax.rem(t, 3))), work)

    def far_blocks(work):
        blocks(0, 4, lambda t: (2, t), work)
        blocks(0, 3, lambda t: (skip_two(t), 2), work)

    def compress(group, yy, xx, at):
        rows = [
            pl.ds(pl.multiple_of(dp_at(zz, yy, xx) * OWN + group * ROWS, ROWS), ROWS)
            for zz in range(NZ)
        ]
        pair = (0, 1)
        combined = [
            [
                unpacked(mom[2 * group + i, at[i] + zz]) + own_g[rows[zz], parts[i].columns]
                for i in pair
            ]
            for zz in range(NZ)
        ]
        scales = []
        for zz in range(NZ):
            size = jnp.abs(combined[zz][0]) + jnp.abs(combined[zz][1])
            total = jnp.sum(size, axis=1, keepdims=True)
            scales.append(total * (1.0 / WIDTH) + tiny_scale)
        for zz in range(NZ):
            inverse = 1.0 / scales[zz]
            for i in pair:
                codes = jnp.clip(combined[zz][i] * inverse, -1.0, 1.0).astype(BF16)
                decoded = codes.astype(F32) * scales[zz]
                left_v[rows[zz], parts[i].columns] = combined[zz][i] - decoded
                dec[2 * group + i, at[i] + zz] = packed(decoded)

    near_rows = (0, 3, 1)
    for group, (gs, rs) in enumerate(zip(by_group(gathers), by_group(reduces))):
        work = functools.partial(compress, group)
        here(gs, near_rows)
        near_blocks(work)
        for row in (3, 1, 0):
            for r in rs:
                r.last(row, 1)
                r.last(row, 3)
        here(gs, (2,))
        far_blocks(work)
        for row in (2, 3, 1, 0):
            for r in rs:
                r.last(row, 2)
                if row == 2:
                    r.last(row, 1)
                    r.last(row, 3)

    for rs in by_group(reduces):

        @pl.loop(0, RING - 1)
        def _(t):
            row = lax.rem(2 + t, RING) + t // 2
            for r in rs:
                r.mid(row)

        for r in rs:
            r.mid_own()
    for rs in by_group(reduces):
        for r in rs:
            r.first(dp_z)

    load_serr.wait()
    load_master.wait()
    load_variance.wait()

    all_codes, all_scales = [], []
    for group, (gs, rs) in enumerate(zip(by_group(gathers_w), by_group(reduces))):
        rows = parts[2 * group].rows
        shifted = [
            unpacked_sum(r.total()) * (1.0 / (NX * NY * NZ)) + serr_v[rows, r.part.columns]
            for r in rs
        ]
        size = jnp.abs(shifted[0]) + jnp.abs(shifted[1])
        scale = jnp.sum(size, axis=1, keepdims=True) * (1.0 / WIDTH) + tiny_scale
        for i, g in enumerate(gs):
            columns = g.part.columns
            codes = jnp.clip(shifted[i] / scale, -1.0, 1.0).astype(BF16).astype(F32)
            all_codes.append(codes)
            momentum = codes * scale
            server_out[rows, columns] = shifted[i] - momentum
            new = master_v[rows, columns] - learn_rate * momentum / (
                jnp.sqrt(variance_v[rows, columns]) + tiny_root
            )
            master_out[rows, columns] = new
            g.part.shard(g.buf, g.part.p, g.part.q, z)[...] = packed(new)
            g.first(dp_z)
        all_scales.append(scale)
    for i in range(2):
        codes_out[:, parts[i].columns] = jnp.concatenate(all_codes[i::2], axis=0).astype(BF16)
    scale = jnp.concatenate(all_scales, axis=0)
    scale_out[...] = jnp.sum(
        jnp.where(eye, jnp.broadcast_to(scale, (OWN, OWN)), 0.0), axis=0, keepdims=True
    )

    @pl.loop(0, HALF // 64)
    def _(t):
        rows = pl.ds(pl.multiple_of(t * 64, 64), 64)
        left_out[rows] = left_v[rows].astype(BF16)

    def assemble(yy, xx, at):
        for zz in range(NZ):
            for i in range(2):
                rows = [unpacked(wts[2 * group + i, at[i] + zz]) for group in range(GROUPS)]
                weights_out[zz, yy, xx, :, parts[i].columns] = jnp.concatenate(
                    rows, axis=0
                ).astype(BF16)

    begin(gathers_w)
    for gs in by_group(gathers_w):
        spread(gs)
    here(gathers_w, near_rows)
    near_blocks(assemble)
    here(gathers_w, (2,))
    far_blocks(assemble)
    for g in gathers + gathers_w + reduces:
        g.drain()
    pltpu.make_async_copy(peer_tx, peer_tx, peer_send.at[0]).wait()


def copy_kernel(count, *refs):
    sources, targets, sems = refs[:count], refs[count : 2 * count], refs[-1]
    copies = [pltpu.make_async_copy(sources[i], targets[i], sems.at[i]) for i in range(count)]
    for copy in copies:
        copy.start()
    for copy in copies:
        copy.wait()


def copied(arrays):
    return pl.pallas_call(
        functools.partial(copy_kernel, len(arrays)),
        out_shape=[jax.ShapeDtypeStruct(a.shape, a.dtype) for a in arrays],
        in_specs=[pl.BlockSpec(memory_space=pltpu.VMEM)] * len(arrays),
        out_specs=[pl.BlockSpec(memory_space=pltpu.HBM)] * len(arrays),
        scratch_shapes=[pltpu.SemaphoreType.DMA((len(arrays),))],
        compiler_params=pltpu.CompilerParams(vmem_limit_bytes=16 * 1024 * 1024),
        name="hand_out",
    )(*arrays)


def body(act, grads, werr, mcodes, mscale, serr, master, variance):
    tokens = act.shape[0]
    hbm = pl.BlockSpec(memory_space=pltpu.HBM)
    vmem = pl.BlockSpec(memory_space=pltpu.VMEM)
    shards = NX * NY * NZ
    tile = (OWN, LANES)
    count = 2 * GROUPS

    def vm(*shape, dtype=BF16):
        return pltpu.VMEM(shape, dtype)

    scratch = [
        vm(2 * CHUNKS, tokens, CHUNK),
        vm(tokens, WIDTH),
        vm(HALF, WIDTH),
        vm(OWN, WIDTH),
        vm(OWN, WIDTH, dtype=F32),
        vm(OWN, WIDTH, dtype=F32),
        vm(OWN, WIDTH, dtype=F32),
        vm(HALF, WIDTH, dtype=F32),
        vm(HALF, WIDTH, dtype=F32),
        vm(HALF, WIDTH),
        vm(HALF, WIDTH),
        vm(count, shards, *tile),
        vm(count, shards, *tile),
        vm(count, shards, *tile),
        vm(count, RING, (RING - 1) * NZ, *tile),
        vm(count, RING, NZ, *tile),
        vm(count, (RING - 1) * NZ, *tile),
        vm(count, NZ, *tile, dtype=F32),
        vm(count, NZ, *tile),
        vm(count, NZ - 1, *tile),
    ]
    dma = pltpu.SemaphoreType.DMA
    scratch += [
        dma((6,)),
        dma((2 * CHUNKS,)),
        dma((1,)),
        dma((1,)),
        dma((3 * count,)),
        dma((2 * count * G_COUNT + count * R_COUNT,)),
    ]
    shape = pltpu.VMEM
    outs = pl.pallas_call(
        step_kernel,
        out_shape=[
            shape((HALF, WIDTH), BF16),
            shape((OWN, WIDTH), BF16),
            shape((1, OWN), F32),
            shape((OWN, WIDTH), F32),
            shape((OWN, WIDTH), F32),
            shape((NZ, NY, NX, OWN, WIDTH), BF16),
        ],
        in_specs=[hbm] * 4 + [vmem] + [hbm] * 3,
        out_specs=[vmem] * 6,
        scratch_shapes=scratch,
        compiler_params=pltpu.CompilerParams(
            collective_id=0, has_side_effects=True, vmem_limit_bytes=54 * 1024 * 1024
        ),
        cost_estimate=pl.CostEstimate(
            flops=2 * tokens * 2 * HALF * WIDTH, bytes_accessed=14_000_000, transcendentals=0
        ),
        name="adam_step",
    )(act, grads, werr[0], mcodes, mscale.reshape(1, OWN), serr, master, variance)
    outs = [*outs[:-1], outs[-1].reshape(HALF, WIDTH)]
    left, codes, scale, server, new_master, weights = copied(outs)
    return (
        left[None],
        codes,
        scale.reshape(OWN),
        server,
        new_master,
        weights,
    )


def solution(mesh):
    return jax.shard_map(
        body,
        mesh=mesh,
        in_specs=(
            P(("dp", "rep"), None),
            P(("dp", "rep"), None),
            P("dp", "rep", None),
            P(("rep", "dp"), None),
            P(("rep", "dp")),
            P(("rep", "dp"), None),
            P(("rep", "dp"), None),
            P(("rep", "dp"), None),
        ),
        out_specs=(
            P("dp", "rep", None),
            P(("rep", "dp"), None),
            P(("rep", "dp")),
            P(("rep", "dp"), None),
            P(("rep", "dp"), None),
            P("rep", None),
        ),
        check_vma=False,
    )
```

```python
import functools
import math

import jax
import jax.numpy as jnp
from jax import lax
from jax.experimental import pallas as pl
from jax.experimental.pallas import tpu as pltpu
from jax.sharding import PartitionSpec as P

BF16 = jnp.bfloat16
F32 = jnp.float32
MESH = pl.DeviceIdType.MESH

NX, NY, NZ = 4, 4, 8
RING = 4
OWN = 16
GROUPS = 2
ROWS = OWN // GROUPS
PART = 256
LANES = PART // GROUPS
CHUNK = 256
HALF = 2048
WIDTH = 512
CHUNKS = HALF // CHUNK

beta_one = 0.9
learn_rate = 0.02
grad_boost = 8.0
tiny_scale = 1e-06
tiny_root = 1e-08


class Part:
    def __init__(self, group, column, p, q, dp_pq, core, send_sems, recv_sems):
        self.rows = slice(group * ROWS, (group + 1) * ROWS)
        self.columns = slice(column, column + PART)
        self.p, self.q, self.dp_pq, self.core = p, q, dp_pq, core
        self.send_sems, self.recv_sems = send_sems, recv_sems

    def at_p(self, k):
        return lax.rem(self.p + (k + RING), RING)

    def at_q(self, k):
        return lax.rem(self.q + (k + RING), RING)

    def shard(self, buf, p, q, z):
        return buf.at[(p * RING + q) * NZ + z]

    def block(self, buf, p, q):
        return buf.at[pl.ds((p * RING + q) * NZ, NZ)]

    def half(self, buf, p, q, which):
        return buf.at[pl.ds((p * RING + q) * NZ + which * (NZ // 2), NZ // 2)]

    def send(self, src, dst, send, recv, dp):
        pltpu.make_async_remote_copy(
            src_ref=src,
            dst_ref=dst,
            send_sem=self.send_sems.at[send],
            recv_sem=self.recv_sems.at[recv],
            device_id={"dp": dp, "rep": self.core},
            device_id_type=MESH,
        ).start()

    def wait(self, like, recv):
        pltpu.make_async_copy(like, like, self.recv_sems.at[recv]).wait()

    def drain(self, like, send):
        pltpu.make_async_copy(like, like, self.send_sems.at[send]).wait()


G_FIRST, G_MID, G_ROW, G_LEFT, G_RIGHT, G_COUNT = 0, 0, 4, 8, 9, 10
R_FIRST, R_MID, R_ROW, R_COUNT = 0, 1, 2, 6


def packed(rows):
    return jnp.concatenate([rows[:, :LANES], rows[:, LANES:]], axis=0).astype(BF16)


def unpacked_sum(wide):
    return jnp.concatenate([wide[:ROWS], wide[ROWS:]], axis=1)


def unpacked(tile):
    return unpacked_sum(tile.astype(F32))


NEAR = (0,)


class Gather:
    def __init__(self, part, buf, z, send, recv):
        self.part, self.buf, self.z, self.send_sem, self.recv = part, buf, z, send, recv

    def go(self, src, dst_recv, dp):
        self.part.send(src, src, self.send_sem, self.recv + dst_recv, dp)

    def first(self, dp_z):
        mine = self.part.shard(self.buf, self.part.p, self.part.q, self.z)
        for k in (4, 3, 5, 2, 6, 1, 7):
            self.go(mine, G_FIRST, dp_z(lax.rem(self.z + k, NZ)))

    def first_here(self):
        self.part.wait(self.buf.at[pl.ds(0, NZ - 1)], self.recv + G_FIRST)

    def mid(self):
        part = self.part
        for k in (2, 1, 3):
            self.go(part.block(self.buf, part.p, part.q), G_MID + k, part.dp_pq(part.p, part.at_q(k)))

    def mid_here(self, k):
        part = self.part
        part.wait(part.block(self.buf, part.p, part.at_q(-k)), self.recv + G_MID + k)

    def last(self, row):
        part = self.part
        block = part.block(self.buf, part.p, part.at_q(row))
        for k in (2, 1, 3):
            self.go(block, G_ROW + row, part.dp_pq(part.at_p(k), part.q))

    def halves(self, p, row):
        q = self.part.at_q(row)
        return self.part.half(self.buf, p, q, 0), self.part.half(self.buf, p, q, 1)

    def last_near(self, row):
        part = self.part
        lower, upper = self.halves(part.p, row)
        after, before = part.dp_pq(part.at_p(1), part.q), part.dp_pq(part.at_p(-1), part.q)
        slot = NEAR.index(row)
        self.go(lower, G_LEFT + slot, after)
        self.go(upper, G_RIGHT + slot, before)
        self.go(upper, G_ROW + row, after)
        self.go(lower, G_ROW + row, before)

    def relay(self, row):
        part = self.part
        slot = NEAR.index(row)
        lower = self.halves(part.at_p(-1), row)[0]
        part.wait(lower, self.recv + G_LEFT + slot)
        self.go(lower, G_ROW + row, part.dp_pq(part.at_p(1), part.q))
        upper = self.halves(part.at_p(1), row)[1]
        part.wait(upper, self.recv + G_RIGHT + slot)
        self.go(upper, G_ROW + row, part.dp_pq(part.at_p(-1), part.q))

    def row_here(self, row):
        blocks = 3 if row not in NEAR else 2
        self.part.wait(self.buf.at[pl.ds(0, blocks * NZ)], self.recv + G_ROW + row)

    def drain(self):
        self.part.drain(self.buf.at[pl.ds(0, NX * NY * NZ - 1)], self.send_sem)


def begin(gathers):
    for g in gathers:
        g.first_here()
        g.mid()
    for g in gathers:
        g.last_near(0)


def spread(gathers):
    for k in (1, 3):
        for g in gathers:
            g.mid_here(k)
            g.last(RING - k)
    for g in gathers:
        g.relay(0)
    for g in gathers:
        g.mid_here(2)
        g.last(2)


def here(gathers, rows):
    for row in rows:
        for g in gathers:
            g.row_here(row)


class Reduce:
    def __init__(self, part, dec, z, send, recv, far, partial, mids, sums, rounded, firsts):
        self.part, self.dec, self.z, self.send_sem, self.recv = part, dec, z, send, recv
        self.far, self.partial = far, partial
        self.mids, self.sums, self.rounded, self.firsts = mids, sums, rounded, firsts

    def go(self, src, dst, recv, dp):
        self.part.send(src, dst, self.send_sem, self.recv + recv, dp)

    def last(self, row, k):
        part = self.part
        self.go(
            part.block(self.dec, part.at_p(k), part.at_q(row)),
            self.far.at[row, pl.ds((k - 1) * NZ, NZ)],
            R_ROW + row,
            part.dp_pq(part.at_p(k), part.q),
        )

    def row_total(self, row):
        part = self.part
        part.wait(self.far.at[row], self.recv + R_ROW + row)
        total = part.block(self.dec, part.p, part.at_q(row))[...].astype(F32)
        for k in range(RING - 1):
            total += self.far[row, pl.ds(k * NZ, NZ)].astype(F32)
        return total

    def mid(self, row):
        part = self.part
        self.partial[row] = self.row_total(row).astype(BF16)
        self.go(
            self.partial.at[row],
            self.mids.at[pl.ds((row - 1) * NZ, NZ)],
            R_MID,
            part.dp_pq(part.p, part.at_q(row)),
        )

    def mid_own(self):
        self.sums[...] = self.row_total(0)

    def first(self, dp_z):
        self.part.wait(self.mids, self.recv + R_MID)
        total = self.sums[...]
        for k in range(RING - 1):
            total += self.mids[pl.ds(k * NZ, NZ)].astype(F32)
        self.sums[...] = total
        self.rounded[...] = total.astype(BF16)
        for k in range(1, NZ):
            to = lax.rem(self.z + k, NZ)
            self.go(self.rounded.at[to], self.firsts.at[k - 1], R_FIRST, dp_z(to))

    def total(self):
        self.part.wait(self.firsts, self.recv + R_FIRST)
        total = self.sums[self.z]
        for k in range(NZ - 1):
            total += self.firsts[k].astype(F32)
        return total

    def drain(self):
        self.part.drain(self.dec.at[pl.ds(0, NX * NY * NZ - 1)], self.send_sem)


def step_kernel(
    act, grads, werr, mcodes, mscale, serr, master, variance,
    left_out, codes_out, scale_out, server_out, master_out, weights_out,
    act_v, grads_v, werr_v, mcodes_v, serr_v, master_v, variance_v,
    own_g, left_v, peer_tx, peer_rx,
    mom, dec, wts, far, partial, mids, sums, rounded, firsts,
    in_sems, act_sems, peer_send, peer_recv, send_sems, recv_sems,
):
    dp = lax.axis_index("dp")
    core = lax.axis_index("rep")
    x = lax.rem(dp, NX)
    y = lax.rem(dp // NX, NY)
    z = dp // (NX * NY)
    other = 1 - core
    tokens = act.shape[0]
    factor = (1.0 - beta_one) * grad_boost / math.sqrt(2 * tokens)

    def load(k, src, dst):
        copy = pltpu.make_async_copy(src, dst, in_sems.at[k])
        copy.start()
        return copy

    load_codes = load(0, mcodes, mcodes_v)

    def dp_at(zz, yy, xx):
        return zz * (NX * NY) + yy * NX + xx

    def dp_z(zz):
        return dp_at(zz, y, x)

    barrier = pltpu.get_barrier_semaphore()
    peers = [(dp_at(lax.rem(z + k, NZ), y, x), core) for k in range(1, NZ)]
    peers += [(dp_at(z, y, lax.rem(x + k, NX)), core) for k in range(1, NX)]
    peers += [(dp_at(z, lax.rem(y + k, NY), x), core) for k in range(1, NY)]
    peers += [(dp, other)]
    for peer_dp, peer_core in peers:
        pl.semaphore_signal(
            barrier, inc=1, device_id={"dp": peer_dp, "rep": peer_core}, device_id_type=MESH
        )

    load_grads = load(1, grads, grads_v)

    def act_copy(k):
        base = jnp.where(k < CHUNKS, other * HALF, core * HALF)
        column = pl.multiple_of(base + lax.rem(k, CHUNKS) * CHUNK, CHUNK)
        return pltpu.make_async_copy(
            act.at[:, pl.ds(column, CHUNK)], act_v.at[k], act_sems.at[k]
        )

    @pl.loop(0, 2 * CHUNKS)
    def _(k):
        act_copy(k).start()

    load_werr = load(2, werr, werr_v)
    load_serr = load(3, serr, serr_v)
    load_master = load(4, master, master_v)
    load_variance = load(5, variance, variance_v)

    eye = lax.broadcasted_iota(jnp.int32, (OWN, OWN), 0) == lax.broadcasted_iota(
        jnp.int32, (OWN, OWN), 1
    )
    scale_col = jnp.sum(
        jnp.where(eye, jnp.broadcast_to(mscale[...], (OWN, OWN)), 0.0), axis=1, keepdims=True
    )
    load_codes.wait()
    previous = mcodes_v[...].astype(F32) * (beta_one * scale_col)

    def x_major(p, q):
        return dp_at(z, q, p)

    def y_major(p, q):
        return dp_at(z, p, q)

    parts = []
    for group in range(GROUPS):
        parts += [
            Part(group, 0, x, y, x_major, core, send_sems, recv_sems),
            Part(group, PART, y, x, y_major, core, send_sems, recv_sems),
        ]
    count = len(parts)

    def by_group(items):
        return [items[2 * group : 2 * group + 2] for group in range(GROUPS)]

    gathers, gathers_w, reduces = [], [], []
    for n, part in enumerate(parts):
        part.shard(mom.at[n], part.p, part.q, z)[...] = packed(previous[part.rows, part.columns])
        gathers.append(Gather(part, mom.at[n], z, 3 * n, n * G_COUNT))
        gathers_w.append(Gather(part, wts.at[n], z, 3 * n + 2, (count + n) * G_COUNT))
        reduces.append(
            Reduce(
                part, dec.at[n], z, 3 * n + 1, 2 * count * G_COUNT + n * R_COUNT, far.at[n],
                partial.at[n], mids.at[n], sums.at[n], rounded.at[n], firsts.at[n],
            )
        )
    pl.semaphore_wait(barrier, len(peers))
    for g in gathers:
        g.first(dp_z)

    def product(k):
        act_copy(k).wait()
        return lax.dot_general(
            act_v[k], grads_v[...], (((0,), (0,)), ((), ())), preferred_element_type=F32
        )

    def chunk_rows(k):
        return pl.ds(pl.multiple_of(k * CHUNK, CHUNK), CHUNK)

    def peer_copy(k):
        rows = chunk_rows(k)
        return pltpu.make_async_remote_copy(
            src_ref=peer_tx.at[rows],
            dst_ref=peer_rx.at[rows],
            send_sem=peer_send.at[0],
            recv_sem=peer_recv.at[0],
            device_id={"dp": dp, "rep": other},
            device_id_type=MESH,
        )

    load_grads.wait()

    @pl.loop(0, CHUNKS)
    def _(k):
        peer_tx[chunk_rows(k)] = (product(k) * factor).astype(BF16)
        peer_copy(k).start()

    def for_own(lo, hi):
        @pl.loop(lo, hi)
        def _(k):
            rows = chunk_rows(k)
            own_g[rows] = product(k + CHUNKS) * factor + werr_v[rows].astype(F32)

    begin(gathers)
    load_werr.wait()
    for_own(0, 6)
    for gs in by_group(gathers):
        spread(gs)
    for_own(6, 8)
    pltpu.make_async_copy(peer_rx, peer_rx, peer_recv.at[0]).wait()

    @pl.loop(0, HALF // 64)
    def _(t):
        rows = pl.ds(pl.multiple_of(t * 64, 64), 64)
        own_g[rows] += peer_rx[rows].astype(F32)

    def blocks(lo, hi, offsets, work):
        @pl.loop(lo, hi)
        def _(t):
            dx, dy = offsets(t)
            xx, yy = lax.rem(x + dx, NX), lax.rem(y + dy, NY)
            work(yy, xx, [(xx * RING + yy) * NZ, (yy * RING + xx) * NZ])

    def skip_two(k):
        return k + k // 2

    def near_blocks(work):
        blocks(0, 9, lambda t: (skip_two(t // 3), skip_two(lax.rem(t, 3))), work)

    def far_blocks(work):
        blocks(0, 4, lambda t: (2, t), work)
        blocks(0, 3, lambda t: (skip_two(t), 2), work)

    def compress(group, yy, xx, at):
        rows = [
            pl.ds(pl.multiple_of(dp_at(zz, yy, xx) * OWN + group * ROWS, ROWS), ROWS)
            for zz in range(NZ)
        ]
        pair = (0, 1)
        combined = [
            [
                unpacked(mom[2 * group + i, at[i] + zz]) + own_g[rows[zz], parts[i].columns]
                for i in pair
            ]
            for zz in range(NZ)
        ]
        scales = []
        for zz in range(NZ):
            size = jnp.abs(combined[zz][0]) + jnp.abs(combined[zz][1])
            total = jnp.sum(size, axis=1, keepdims=True)
            scales.append(total * (1.0 / WIDTH) + tiny_scale)
        for zz in range(NZ):
            inverse = 1.0 / scales[zz]
            for i in pair:
                codes = jnp.clip(combined[zz][i] * inverse, -1.0, 1.0).astype(BF16)
                decoded = codes.astype(F32) * scales[zz]
                left_v[rows[zz], parts[i].columns] = combined[zz][i] - decoded
                dec[2 * group + i, at[i] + zz] = packed(decoded)

    near_rows = (0, 3, 1)
    for group, (gs, rs) in enumerate(zip(by_group(gathers), by_group(reduces))):
        work = functools.partial(compress, group)
        here(gs, near_rows)
        near_blocks(work)
        for row in (3, 1, 0):
            for r in rs:
                r.last(row, 1)
                r.last(row, 3)
        here(gs, (2,))
        far_blocks(work)
        for row in (2, 3, 1, 0):
            for r in rs:
                r.last(row, 2)
                if row == 2:
                    r.last(row, 1)
                    r.last(row, 3)

    for rs in by_group(reduces):

        @pl.loop(0, RING - 1)
        def _(t):
            row = lax.rem(2 + t, RING) + t // 2
            for r in rs:
                r.mid(row)

        for r in rs:
            r.mid_own()
    for rs in by_group(reduces):
        for r in rs:
            r.first(dp_z)

    load_serr.wait()
    load_master.wait()
    load_variance.wait()

    all_codes, all_scales = [], []
    for group, (gs, rs) in enumerate(zip(by_group(gathers_w), by_group(reduces))):
        rows = parts[2 * group].rows
        shifted = [
            unpacked_sum(r.total()) * (1.0 / (NX * NY * NZ)) + serr_v[rows, r.part.columns]
            for r in rs
        ]
        size = jnp.abs(shifted[0]) + jnp.abs(shifted[1])
        scale = jnp.sum(size, axis=1, keepdims=True) * (1.0 / WIDTH) + tiny_scale
        for i, g in enumerate(gs):
            columns = g.part.columns
            codes = jnp.clip(shifted[i] / scale, -1.0, 1.0).astype(BF16).astype(F32)
            all_codes.append(codes)
            momentum = codes * scale
            server_out[rows, columns] = shifted[i] - momentum
            new = master_v[rows, columns] - learn_rate * momentum / (
                jnp.sqrt(variance_v[rows, columns]) + tiny_root
            )
            master_out[rows, columns] = new
            g.part.shard(g.buf, g.part.p, g.part.q, z)[...] = packed(new)
            g.first(dp_z)
        all_scales.append(scale)
    for i in range(2):
        codes_out[:, parts[i].columns] = jnp.concatenate(all_codes[i::2], axis=0).astype(BF16)
    scale = jnp.concatenate(all_scales, axis=0)
    scale_out[...] = jnp.sum(
        jnp.where(eye, jnp.broadcast_to(scale, (OWN, OWN)), 0.0), axis=0, keepdims=True
    )

    @pl.loop(0, HALF // 64)
    def _(t):
        rows = pl.ds(pl.multiple_of(t * 64, 64), 64)
        left_out[rows] = left_v[rows].astype(BF16)

    def assemble(row):
        @pl.loop(0, RING)
        def _(p):
            for i in range(2):
                q = parts[i].at_q(row)
                xx, yy = (p, q) if i == 0 else (q, p)
                for zz in range(NZ):
                    at = (p * RING + q) * NZ + zz
                    rows = [unpacked(wts[2 * group + i, at]) for group in range(GROUPS)]
                    weights_out[zz, yy, xx, :, parts[i].columns] = jnp.concatenate(
                        rows, axis=0
                    ).astype(BF16)

    begin(gathers_w)
    for gs in by_group(gathers_w):
        spread(gs)
    for row in (*near_rows, 2):
        here(gathers_w, (row,))
        assemble(row)
    for g in gathers + gathers_w + reduces:
        g.drain()
    pltpu.make_async_copy(peer_tx, peer_tx, peer_send.at[0]).wait()


def copy_kernel(count, *refs):
    sources, targets, sems = refs[:count], refs[count : 2 * count], refs[-1]
    copies = [pltpu.make_async_copy(sources[i], targets[i], sems.at[i]) for i in range(count)]
    for copy in copies:
        copy.start()
    for copy in copies:
        copy.wait()


def copied(arrays):
    return pl.pallas_call(
        functools.partial(copy_kernel, len(arrays)),
        out_shape=[jax.ShapeDtypeStruct(a.shape, a.dtype) for a in arrays],
        in_specs=[pl.BlockSpec(memory_space=pltpu.VMEM)] * len(arrays),
        out_specs=[pl.BlockSpec(memory_space=pltpu.HBM)] * len(arrays),
        scratch_shapes=[pltpu.SemaphoreType.DMA((len(arrays),))],
        compiler_params=pltpu.CompilerParams(vmem_limit_bytes=16 * 1024 * 1024),
        name="hand_out",
    )(*arrays)


def body(act, grads, werr, mcodes, mscale, serr, master, variance):
    tokens = act.shape[0]
    hbm = pl.BlockSpec(memory_space=pltpu.HBM)
    vmem = pl.BlockSpec(memory_space=pltpu.VMEM)
    shards = NX * NY * NZ
    tile = (OWN, LANES)
    count = 2 * GROUPS

    def vm(*shape, dtype=BF16):
        return pltpu.VMEM(shape, dtype)

    scratch = [
        vm(2 * CHUNKS, tokens, CHUNK),
        vm(tokens, WIDTH),
        vm(HALF, WIDTH),
        vm(OWN, WIDTH),
        vm(OWN, WIDTH, dtype=F32),
        vm(OWN, WIDTH, dtype=F32),
        vm(OWN, WIDTH, dtype=F32),
        vm(HALF, WIDTH, dtype=F32),
        vm(HALF, WIDTH, dtype=F32),
        vm(HALF, WIDTH),
        vm(HALF, WIDTH),
        vm(count, shards, *tile),
        vm(count, shards, *tile),
        vm(count, shards, *tile),
        vm(count, RING, (RING - 1) * NZ, *tile),
        vm(count, RING, NZ, *tile),
        vm(count, (RING - 1) * NZ, *tile),
        vm(count, NZ, *tile, dtype=F32),
        vm(count, NZ, *tile),
        vm(count, NZ - 1, *tile),
    ]
    dma = pltpu.SemaphoreType.DMA
    scratch += [
        dma((6,)),
        dma((2 * CHUNKS,)),
        dma((1,)),
        dma((1,)),
        dma((3 * count,)),
        dma((2 * count * G_COUNT + count * R_COUNT,)),
    ]
    shape = pltpu.VMEM
    outs = pl.pallas_call(
        step_kernel,
        out_shape=[
            shape((HALF, WIDTH), BF16),
            shape((OWN, WIDTH), BF16),
            shape((1, OWN), F32),
            shape((OWN, WIDTH), F32),
            shape((OWN, WIDTH), F32),
            shape((NZ, NY, NX, OWN, WIDTH), BF16),
        ],
        in_specs=[hbm] * 4 + [vmem] + [hbm] * 3,
        out_specs=[vmem] * 6,
        scratch_shapes=scratch,
        compiler_params=pltpu.CompilerParams(
            collective_id=0, has_side_effects=True, vmem_limit_bytes=54 * 1024 * 1024
        ),
        cost_estimate=pl.CostEstimate(
            flops=2 * tokens * 2 * HALF * WIDTH, bytes_accessed=14_000_000, transcendentals=0
        ),
        name="adam_step",
    )(act, grads, werr[0], mcodes, mscale.reshape(1, OWN), serr, master, variance)
    outs = [*outs[:-1], outs[-1].reshape(HALF, WIDTH)]
    left, codes, scale, server, new_master, weights = copied(outs)
    return (
        left[None],
        codes,
        scale.reshape(OWN),
        server,
        new_master,
        weights,
    )


def solution(mesh):
    return jax.shard_map(
        body,
        mesh=mesh,
        in_specs=(
            P(("dp", "rep"), None),
            P(("dp", "rep"), None),
            P("dp", "rep", None),
            P(("rep", "dp"), None),
            P(("rep", "dp")),
            P(("rep", "dp"), None),
            P(("rep", "dp"), None),
            P(("rep", "dp"), None),
        ),
        out_specs=(
            P("dp", "rep", None),
            P(("rep", "dp"), None),
            P(("rep", "dp")),
            P(("rep", "dp"), None),
            P(("rep", "dp"), None),
            P("rep", None),
        ),
        check_vma=False,
    )
```
